256 devices in a mesh: tok: 8 (over z), feat: 32 (over x, y, core).
Axes of the slice: x: 4, y: 4, z: 8, core: 2. Of those that a mesh axis runs over, the one named last changes fastest.
Arguments:
- features: float32 [8192, 65536], P('tok', 'feat'), may hold values from -54 to 54
- labels: int32 [8192], P('tok'), may hold values from 0 to 15
- weights: float32 [16, 65536], P(None, 'feat'), may hold values from -0.0234375 to 0.0234375
- right_side: float32 [16, 65536], P(None, 'feat'), may hold values from -6 to 6
Outputs:
- solution: float32 [16, 65536], P(None, 'feat')
- residual: float32 [16, 65536], P(None, 'feat')
The draws below stay inside these ranges and needn't reach their ends.
All inputs are finite; a program needn't handle non-finite values.
Results may differ from the reference program's by a relative error of at most 0.00035.
Values sent between devices are 32-bit elements; how exact they have to be, the bound alone decides.
No kernel may reach another device: no remote copies, remote signals or barrier semaphores. Data moves between devices by JAX's collectives and lax.ppermute only.
A program may use at most 64 MiB of HBM per device.

```python
import math
import jax
import jax.numpy as jnp
from jax import lax

F = 65536
C = 16
TOKENS = 8192
ITERS = 2


def draw_features(key, part):
    key = jax.random.fold_in(key, 11)
    first, second, third = jax.random.split(key, 3)
    base = jnp.clip(jax.random.normal(first, (TOKENS, F), jnp.float32), -6.0, 6.0)
    row_scale = jnp.exp(jax.random.uniform(second, (TOKENS, 1), jnp.float32, math.log(0.5), math.log(3.0)))
    column_scale = jnp.exp(jax.random.uniform(third, (1, F), jnp.float32, math.log(0.3), math.log(3.0)))
    return base * row_scale * column_scale


def draw_labels(key, part):
    key = jax.random.fold_in(key, 23)
    first, second, third = jax.random.split(key, 3)
    position = jnp.arange(TOKENS, dtype=jnp.int32)
    lower = jax.random.randint(first, (TOKENS,), 0, 8, dtype=jnp.int32)
    upper = jax.random.randint(second, (TOKENS,), 8, 16, dtype=jnp.int32)
    chooser = jax.random.randint(third, (TOKENS,), 0, 5 * TOKENS, dtype=jnp.int32)
    return jnp.where(chooser < TOKENS + 3 * position, lower, upper).astype(jnp.int32)


def steps_of(rng, extent, pieces, low, high):
    level = 1.0
    for dim, parts in pieces:
        heights = jax.random.uniform(jax.random.fold_in(jax.random.fold_in(rng, 6), dim), (parts,), jnp.float32, low / len(pieces), high / len(pieces))
        level = level * jnp.repeat(jnp.exp(heights), extent[dim] // parts).reshape((-1,) + (1,) * (len(extent) - 1 - dim))
    return level


def noise(own_key, shape, width, reach, cuts=(), kind=jnp.bfloat16):
    values = jax.random.normal(own_key, shape, jnp.float32) * width
    if len(cuts) > 0:
        values = steps_of(own_key, shape, cuts, -0.22, 0.18) * values
    return jnp.clip(values, min=-reach, max=reach).astype(kind)


def setup_inputs(seed: int = 0) -> dict:
    keys = jax.random.split(jax.random.key(seed), 5)
    features = draw_features(jax.random.fold_in(keys[4], 71), 0)
    labels = draw_labels(jax.random.fold_in(keys[4], 71), 0)
    weights = noise(keys[2], (C, F), F ** -0.5, 0.0234375, ((1, 32),), jnp.float32)
    right_side = noise(keys[3], (C, F), 1.0, 6.0, ((1, 32),), jnp.float32)
    return {"features": features, "labels": labels, "weights": weights, "right_side": right_side}


ridge_strength = 0.25


def against(left, slab):
    return lax.dot_general(left, slab, (((1,), (1,)), ((), ())), precision=lax.Precision.HIGHEST, preferred_element_type=jnp.float32)


def reference(features, labels, weights, right_side):
    classes = jnp.arange(C, dtype=jnp.int32)
    onehot = (labels[None, :] == classes[:, None]).astype(jnp.float32)
    counts = jnp.sum(onehot, axis=1)
    token_scale = 1.0 / (C * jnp.sum(onehot * counts[:, None], axis=0))
    logits = against(weights, features)
    powered = jnp.exp(logits)
    probabilities = powered / jnp.sum(powered, axis=0, keepdims=True)

    def hessian(vector):
        projected = against(vector, features)
        average = jnp.sum(probabilities * projected, axis=0, keepdims=True)
        weighted = token_scale[None, :] * probabilities * (projected - average)
        data_part = jnp.dot(weighted, features, precision=lax.Precision.HIGHEST, preferred_element_type=jnp.float32)
        return data_part + ridge_strength * vector

    solution = jnp.zeros_like(right_side)
    residual = right_side
    direction = right_side
    norm_now = jnp.sum(residual * residual)
    for iteration in range(ITERS):
        image = hessian(direction)
        step_size = norm_now / jnp.sum(direction * image)
        solution = solution + step_size * direction
        residual = residual - step_size * image
        if iteration + 1 < ITERS:
            norm_next = jnp.sum(residual * residual)
            direction = residual + (norm_next / norm_now) * direction
            norm_now = norm_next
    return solution, residual
```

```python
import jax
import jax.numpy as jnp
from jax import lax
from jax.sharding import Mesh, PartitionSpec as P

ridge_strength = 0.25
three_pass = lax.Precision.HIGH


def on_device(features, labels, weights, right_side):
    classes, width = weights.shape
    tokens = features.shape[0]
    half = tokens // 2
    core = lax.axis_index("core")
    toks = lax.axis_size("tok")
    chips = lax.axis_size("chip")
    swap = [(0, 1), (1, 0)]

    def scalars_row(columns, *values):
        row = jnp.stack(values)[None, :]
        return jnp.pad(row, ((0, 7), (0, columns - row.shape[1])))

    def sum_over_feat(part, *values):
        tail = scalars_row(half, *values)
        mine = lax.dynamic_slice_in_dim(part, core * half, half, axis=1)
        other = lax.dynamic_slice_in_dim(part, (1 - core) * half, half, axis=1)
        other = jnp.concatenate([other, tail])
        mine = jnp.concatenate([mine, tail])
        both = mine + lax.ppermute(other, "core", swap)
        spread = jnp.broadcast_to(both[None], (chips,) + both.shape)
        total = jnp.sum(lax.all_to_all(spread, "chip", 0, 0), axis=0)
        rows = part.shape[0]
        return total[:rows], [total[rows, i] for i in range(len(values))]

    def sum_over_tok(part, value):
        step = width // toks
        pieces = part.reshape(classes, toks, step).transpose(1, 0, 2)
        piece = jnp.sum(lax.all_to_all(pieces, "tok", 0, 0), axis=0)
        piece = jnp.concatenate([piece, scalars_row(step, value)])
        spread = jnp.broadcast_to(piece[None], (toks,) + piece.shape)
        pieces = lax.all_to_all(spread, "tok", 0, 0)
        whole = pieces[:, :classes].transpose(1, 0, 2).reshape(classes, width)
        return whole, jnp.sum(pieces[:, classes, 0])

    def product(left, contract):
        return lax.dot_general(
            left, features, (((1,), (contract,)), ((), ())), precision=three_pass, preferred_element_type=jnp.float32
        )

    class_ids = jnp.arange(classes, dtype=jnp.int32)
    onehot = (labels[None, :] == class_ids[:, None]).astype(jnp.float32)
    counts = jnp.sum(onehot, axis=1)
    counts = jnp.broadcast_to(counts[None, :], (8, classes))
    total = counts
    for shift in range(1, toks):
        total = total + lax.ppermute(counts, "tok", [(i, (i + shift) % toks) for i in range(toks)])
    counts = total[0]
    onehot_half = lax.dynamic_slice_in_dim(onehot, core * half, half, axis=1)
    token_scale = 1.0 / (classes * jnp.sum(onehot_half * counts[:, None], axis=0))

    part = product(jnp.concatenate([weights, right_side]), 1)
    total, (norm_now,) = sum_over_feat(part, jnp.sum(right_side * right_side))
    logits, first = total[:classes], total[classes:]
    powered = jnp.exp(logits)
    probabilities = powered / jnp.sum(powered, axis=0, keepdims=True)

    def apply(projected):
        average = jnp.sum(probabilities * projected, axis=0, keepdims=True)
        weighted = token_scale[None, :] * probabilities * (projected - average)
        curve = jnp.sum(projected * weighted)
        packed = jnp.concatenate([weighted, scalars_row(half, curve)])
        other = lax.ppermute(packed, "core", swap)
        low = jnp.where(core == 0, weighted, other[:classes])
        high = jnp.where(core == 0, other[:classes], weighted)
        return sum_over_tok(product(jnp.concatenate([low, high], axis=1), 0), curve + other[classes, 0])

    data, curve = apply(first)
    step_size = norm_now / (curve + ridge_strength * norm_now)
    solution = step_size * right_side
    residual = right_side - step_size * (data + ridge_strength * right_side)

    part = product(residual, 1)
    projected, (norm_next, cross) = sum_over_feat(part, jnp.sum(residual * residual), jnp.sum(residual * right_side))
    ratio = norm_next / norm_now
    direction = residual + ratio * right_side
    data, curve = apply(projected + ratio * first)
    norm_direction = norm_next + ratio * (2.0 * cross + ratio * norm_now)
    step_size = norm_next / (curve + ridge_strength * norm_direction)
    solution = solution + step_size * direction
    residual = residual - step_size * (data + ridge_strength * direction)
    return solution, residual


def solution(mesh):
    toks, feats = mesh.devices.shape
    split = Mesh(mesh.devices.reshape(toks, feats // 2, 2), ("tok", "chip", "core"))
    feat = ("chip", "core")
    return jax.shard_map(
        on_device,
        mesh=split,
        in_specs=(P("tok", feat), P("tok"), P(None, feat), P(None, feat)),
        out_specs=(P(None, feat), P(None, feat)),
        check_vma=False,
    )
```

```python
import functools
import math

import jax
import jax.numpy as jnp
from jax import lax
from jax.experimental import pallas as pl
from jax.experimental.pallas import tpu as pltpu
from jax.sharding import Mesh, PartitionSpec as P

ridge_strength = 0.25
SUB, LANE = 8, 128
f32, bf16 = jnp.float32, jnp.bfloat16
ROWS_WITH_ROWS = (((1,), (1,)), ((), ()))
ROWS_WITH_COLUMNS = (((1,), (0,)), ((), ()))
ON_CHIP = pl.BlockSpec(memory_space=pltpu.VMEM)
SCALAR = pl.BlockSpec(memory_space=pltpu.SMEM)
IN_HBM = pl.BlockSpec(memory_space=pltpu.HBM)


def call(kernel, name, in_specs, outs, scratch=(), mib=8, cost=None):
    return pl.pallas_call(
        kernel,
        out_shape=outs,
        in_specs=in_specs,
        out_specs=jax.tree.map(lambda _: ON_CHIP, outs),
        scratch_shapes=list(scratch),
        compiler_params=pltpu.CompilerParams(vmem_limit_bytes=mib << 20),
        cost_estimate=cost,
        name=name,
    )


def tiles(*lead):
    return pltpu.VMEM(lead + (SUB, LANE), f32)


def parts(x):
    high = x.astype(bf16)
    return high, (x - high.astype(f32)).astype(bf16)


def total(tile):
    return jnp.sum(tile, axis=(0, 1), keepdims=True)


def class_sum(pair):
    return jnp.sum(pair[0] + pair[1], axis=0, keepdims=True)


def fold(array):
    rows, columns = array.shape
    kept = None
    for r in range(rows // SUB):
        for c in range(columns // LANE):
            tile = array[r * SUB : (r + 1) * SUB, c * LANE : (c + 1) * LANE]
            kept = tile if kept is None else kept + tile
    return kept


def store_half(core_ref, half, value, extra, keep_ref, send_ref):
    rows, columns = value.shape
    across = columns // LANE

    def store(ref):
        for r in range(rows // SUB):
            for c in range(across):
                ref[r * across + c] = value[r * SUB : (r + 1) * SUB, c * LANE : (c + 1) * LANE]
        for i, tile in enumerate(extra):
            ref[(rows // SUB) * across + i] = tile

    @pl.when(core_ref[0] == half)
    def _():
        store(keep_ref)

    @pl.when(core_ref[0] != half)
    def _():
        store(send_ref)


def count_kernel(labels_ref, spread_ref):
    copies, groups = spread_ref.shape[:2]
    ids = lax.broadcasted_iota(jnp.int32, (SUB, LANE), 0)
    for r in range(groups):
        count = jnp.zeros((SUB, LANE), f32)
        for row in range(labels_ref.shape[0]):
            count += (labels_ref[row : row + 1, :] == ids + r * SUB).astype(f32)
        for i in range(copies):
            spread_ref[i, r] = count


def first_kernel(
    step, core_ref, weights_ref, right_ref, features_ref, order_ref, keep_ref, send_ref, left_ref, block_ref, sems
):
    tokens, width = features_ref.shape
    half = tokens // 2
    across = width // step
    copies = []
    for h in range(2):
        for k in range(across):
            i = h * across + k
            copies.append(
                pltpu.make_async_copy(
                    features_ref.at[pl.ds(h * half, half), pl.ds(k * step, step)], block_ref.at[i], sems.at[i]
                )
            )
            copies[-1].start()
    classes = weights_ref.shape[0]
    rows = 2 * classes
    for i, ref in enumerate((weights_ref, right_ref)):
        high, low = parts(ref[...])
        left_ref[i * classes : (i + 1) * classes] = high
        left_ref[rows + i * classes : rows + (i + 1) * classes] = low
    right = right_ref[...]
    norm = fold(right * right)
    for h in range(2):
        both = jnp.zeros((2 * rows, half), f32)
        rest = jnp.zeros((rows, half), f32)
        for k in range(across):
            i = h * across + k
            part = slice(k * step, (k + 1) * step)
            copies[i].wait()
            high, low = parts(block_ref[i])
            both += lax.dot_general(left_ref[:, part], high, ROWS_WITH_ROWS, preferred_element_type=f32)
            rest += lax.dot_general(left_ref[:rows, part], low, ROWS_WITH_ROWS, preferred_element_type=f32)
        store_half(core_ref, h, both[:rows] + both[rows:] + rest, [norm], keep_ref, send_ref)


def spread_kernel(keep_ref, got_ref, spread_ref):
    value = keep_ref[...] + got_ref[...]
    for i in range(spread_ref.shape[0]):
        spread_ref[i] = value


def spread_first_kernel(keep_ref, got_ref, counts_ref, spread_ref, total_ref):
    spread_kernel(keep_ref, got_ref, spread_ref)
    for r in range(total_ref.shape[0]):
        total_ref[r] = jnp.broadcast_to(jnp.sum(summed(counts_ref, r), axis=1, keepdims=True), (SUB, LANE))


def spread_again_kernel(pieces_ref, spread_ref):
    for k in range(pieces_ref.shape[1]):
        tile = summed(pieces_ref, k)
        for i in range(spread_ref.shape[0]):
            spread_ref[i, k] = tile


def gather_kernel(pieces_ref, extra_ref, spread_ref):
    copies, count = pieces_ref.shape[:2]
    for k in range(count):
        tile = pieces_ref[0, k]
        for i in range(1, copies):
            tile += pieces_ref[i, k]
        for i in range(copies):
            spread_ref[i, k] = tile
    for i in range(copies):
        spread_ref[i, count] = extra_ref[...]


def summed(pieces_ref, k):
    tile = pieces_ref[0, k]
    for i in range(1, pieces_ref.shape[0]):
        tile += pieces_ref[i, k]
    return tile


def weigh(c, across, projected, probability, scaled, weighted_ref):
    average = class_sum([projected[r] * probability[r] for r in range(2)])
    curve = jnp.zeros((SUB, LANE), f32)
    for r in range(2):
        value = scaled[r] * (projected[r] - average)
        weighted_ref[r * across + c] = value
        curve += projected[r] * value
    return curve


def softmax_kernel(
    core_ref, labels_ref, counts_ref, pieces_ref, probability_ref, scaled_ref, first_ref, norm_ref, weighted_ref
):
    across = first_ref.shape[0] // 2
    classes = 2 * SUB
    ids = lax.broadcasted_iota(jnp.int32, (SUB, LANE), 0)
    counts = [counts_ref[r] for r in range(2)]
    curve = jnp.zeros((SUB, LANE), f32)
    for c in range(across):
        powered = [jnp.exp(summed(pieces_ref, r * across + c)) for r in range(2)]
        projected = [summed(pieces_ref, (2 + r) * across + c) for r in range(2)]
        whole = class_sum(powered)
        probability = [powered[r] / whole for r in range(2)]
        label = labels_ref[pl.ds(core_ref[0] * across + c, 1), :]
        own = class_sum([jnp.where(label == ids + r * SUB, counts[r], 0.0) for r in range(2)])
        scale = 1.0 / (classes * own)
        scaled = [scale * probability[r] for r in range(2)]
        for r in range(2):
            probability_ref[r * across + c] = probability[r]
            scaled_ref[r * across + c] = scaled[r]
            first_ref[r * across + c] = projected[r]
        curve += weigh(c, across, projected, probability, scaled, weighted_ref)
    weighted_ref[2 * across] = curve
    norm_ref[...] = jnp.broadcast_to(total(summed(pieces_ref, 4 * across)), (SUB, LANE))


def second_kernel(pieces_ref, probability_ref, scaled_ref, first_ref, norm_ref, weighted_ref, numbers_ref):
    across = first_ref.shape[0] // 2
    sums = summed(pieces_ref, 2 * across)
    norm_next, cross = total(sums[:4]), total(sums[4:])
    norm_now = norm_ref[0:1, 0:1]
    ratio = norm_next / norm_now
    curve = jnp.zeros((SUB, LANE), f32)
    for c in range(across):
        projected, probability, scaled = [], [], []
        for r in range(2):
            i = r * across + c
            projected.append(summed(pieces_ref, i) + ratio * first_ref[i])
            probability.append(probability_ref[i])
            scaled.append(scaled_ref[i])
        curve += weigh(c, across, projected, probability, scaled, weighted_ref)
    weighted_ref[2 * across] = curve
    norm_direction = norm_next + ratio * (2.0 * cross + ratio * norm_now)
    for i, value in enumerate((norm_next, ratio, norm_direction)):
        numbers_ref[i] = jnp.broadcast_to(value, (SUB, LANE))


def put_together(core_ref, own_ref, other_ref, curve_ref, left_ref):
    across = (own_ref.shape[0] - 1) // 2
    classes = 2 * SUB
    half = across * LANE
    mine = core_ref[0] == 0
    for r in range(2):
        for c in range(across):
            own, other = own_ref[r * across + c], other_ref[r * across + c]
            for h, value in enumerate((jnp.where(mine, own, other), jnp.where(mine, other, own))):
                high, low = parts(value)
                at = slice(h * half + c * LANE, h * half + (c + 1) * LANE)
                left_ref[r * SUB : (r + 1) * SUB, at] = high.astype(f32)
                left_ref[classes + r * SUB : classes + (r + 1) * SUB, at] = low.astype(f32)
    curve_ref[...] = own_ref[2 * across] + other_ref[2 * across]
    return left_ref[...].astype(bf16)


def image_columns(k, step, left, high_ref, low_ref, pieces_ref):
    classes = left.shape[0] // 2
    share = pieces_ref.shape[1] // 2
    per = share * LANE
    part = slice(k * step, (k + 1) * step)
    both = lax.dot_general(left, high_ref[:, part], ROWS_WITH_COLUMNS, preferred_element_type=f32)
    rest = lax.dot_general(left[:classes], low_ref[:, part], ROWS_WITH_COLUMNS, preferred_element_type=f32)
    value = both[:classes] + both[classes:] + rest
    for z in range(step // per):
        for r in range(2):
            for c in range(share):
                at = z * per + c * LANE
                pieces_ref[k * (step // per) + z, r * share + c] = value[r * SUB : (r + 1) * SUB, at : at + LANE]


def image_kernel(step, core_ref, own_ref, other_ref, high_ref, low_ref, pieces_ref, curve_ref, left_ref):
    left = put_together(core_ref, own_ref, other_ref, curve_ref, left_ref)
    for k in range(high_ref.shape[1] // step):
        image_columns(k, step, left, high_ref, low_ref, pieces_ref)


def image_first_kernel(
    step, core_ref, own_ref, other_ref, features_ref, pieces_ref, curve_ref, high_ref, low_ref, left_ref, block_ref, sems
):
    copies = []
    for k in range(high_ref.shape[1] // step):
        copies.append(
            pltpu.make_async_copy(features_ref.at[:, pl.ds(k * step, step)], block_ref.at[k], sems.at[k])
        )
        copies[-1].start()
    left = put_together(core_ref, own_ref, other_ref, curve_ref, left_ref)
    for k, copy in enumerate(copies):
        part = slice(k * step, (k + 1) * step)
        copy.wait()
        high_ref[:, part], low_ref[:, part] = parts(block_ref[k])
        image_columns(k, step, left, high_ref, low_ref, pieces_ref)


def columns_of(pieces_ref, z, share, classes):
    rows = []
    for r in range(classes // SUB):
        rows.append(jnp.concatenate([pieces_ref[z, r * share + c] for c in range(share)], axis=1))
    return jnp.concatenate(rows, axis=0)


def residual_kernel(
    core_ref, pieces_ref, norm_ref, right_ref, high_ref, low_ref, keep_ref, send_ref, residual_ref, rate_ref, left_ref
):
    classes, width = right_ref.shape
    toks, count = pieces_ref.shape[:2]
    share = (count - 1) // 2
    per = share * LANE
    norm_now = norm_ref[0:1, 0:1]
    curve = total(summed(pieces_ref, count - 1))
    rate = norm_now / (curve + ridge_strength * norm_now)
    rate_ref[...] = jnp.broadcast_to(rate, (SUB, LANE))
    norm = jnp.zeros((SUB, LANE), f32)
    cross = jnp.zeros((SUB, LANE), f32)
    for z in range(toks):
        at = slice(z * per, (z + 1) * per)
        right = right_ref[:, at]
        residual = right - rate * (columns_of(pieces_ref, z, share, classes) + ridge_strength * right)
        residual_ref[:, at] = residual
        norm += fold(residual * residual)
        cross += fold(residual * right)
        high, low = parts(residual)
        left_ref[:classes, at] = high
        left_ref[classes:, at] = low
    half = high_ref.shape[0] // 2
    left = left_ref[...]
    for h in range(2):
        span = slice(h * half, (h + 1) * half)
        both = lax.dot_general(left, high_ref[span], ROWS_WITH_ROWS, preferred_element_type=f32)
        rest = lax.dot_general(left[:classes], low_ref[span], ROWS_WITH_ROWS, preferred_element_type=f32)
        store_half(core_ref, h, both[:classes] + both[classes:] + rest, [jnp.concatenate([norm[:4] + norm[4:], cross[:4] + cross[4:]])], keep_ref, send_ref)


def last_kernel(pieces_ref, numbers_ref, rate_ref, right_ref, old_ref, solution_ref, residual_ref):
    classes, width = right_ref.shape
    toks, count = pieces_ref.shape[:2]
    share = (count - 1) // 2
    per = share * LANE
    norm_next, ratio, norm_direction = [numbers_ref[i, 0:1, 0:1] for i in range(3)]
    curve = total(summed(pieces_ref, count - 1))
    rate = norm_next / (curve + ridge_strength * norm_direction)
    rate_first = rate_ref[0:1, 0:1]
    for z in range(toks):
        at = slice(z * per, (z + 1) * per)
        right, old = right_ref[:, at], old_ref[:, at]
        direction = old + ratio * right
        image = columns_of(pieces_ref, z, share, classes) + ridge_strength * direction
        solution_ref[:, at] = rate_first * right + rate * direction
        residual_ref[:, at] = old - rate * image


def on_device(features, labels, weights, right_side):
    classes, width = weights.shape
    tokens = features.shape[0]
    half = tokens // 2
    across = half // LANE
    groups = classes // SUB
    toks = lax.axis_size("tok")
    across_x, across_y = lax.axis_size("x"), lax.axis_size("y")
    chips = across_x * across_y
    share = width // toks // LANE
    core = lax.axis_index("core").astype(jnp.int32).reshape(1)
    labels = labels.reshape(tokens // LANE, LANE)
    swap = [(0, 1), (1, 0)]
    step = min(512, width)

    spread = call(count_kernel, "count", [ON_CHIP], tiles(toks, groups))(labels)
    counts = lax.all_to_all(spread, "tok", 0, 0)

    def sum_over_feat(keep, send):
        got = lax.ppermute(send, "core", swap)
        spread = call(spread_kernel, "spread", [ON_CHIP] * 2, tiles(chips, *keep.shape[:1]))(keep, got)
        return lax.all_to_all(spread, ("x", "y"), 0, 0)

    def sum_over_tok(pieces, curve):
        pieces = lax.all_to_all(pieces, "tok", 0, 0)
        spread = call(gather_kernel, "gather", [ON_CHIP] * 2, tiles(toks, groups * share + 1))(pieces, curve)
        return lax.all_to_all(spread, "tok", 0, 0)

    image_outs = [tiles(toks, groups * share), tiles()]
    put = pltpu.VMEM((2 * classes, tokens), f32)
    whole = pltpu.VMEM((tokens, width), bf16)

    kept = 2 * groups * across + 1
    blocks = 2 * (width // step)
    keep, send = call(
        functools.partial(first_kernel, step),
        "first",
        [SCALAR, ON_CHIP, ON_CHIP, IN_HBM, ON_CHIP],
        [tiles(kept), tiles(kept)],
        [
            pltpu.VMEM((4 * classes, width), bf16),
            pltpu.VMEM((blocks, half, step), f32),
            pltpu.SemaphoreType.DMA((blocks,)),
        ],
        mib=48,
        cost=pl.CostEstimate(
            flops=12 * classes * tokens * width, bytes_accessed=4 * tokens * width, transcendentals=0
        ),
    )(core, weights, right_side, features, spread)
    got = lax.ppermute(send, "core", swap)
    spread, counts = call(
        spread_first_kernel, "spread_x", [ON_CHIP] * 3, [tiles(across_x, kept), tiles(groups)]
    )(keep, got, counts)
    pieces = lax.all_to_all(spread, "x", 0, 0)
    spread = call(spread_again_kernel, "spread_y", [ON_CHIP], tiles(across_y, kept))(pieces)
    pieces = lax.all_to_all(spread, "y", 0, 0)
    probability, scaled, first, norm_now, weighted = call(
        softmax_kernel,
        "softmax",
        [SCALAR] + [ON_CHIP] * 3,
        [tiles(groups * across)] * 3 + [tiles(), tiles(groups * across + 1)],
    )(core, labels, counts, pieces)
    pieces, curve, high, low = call(
        functools.partial(image_first_kernel, step),
        "image_first",
        [SCALAR] + [ON_CHIP] * 2 + [IN_HBM],
        image_outs + [whole, whole],
        [put, pltpu.VMEM((width // step, tokens, step), f32), pltpu.SemaphoreType.DMA((width // step,))],
        mib=45,
    )(core, weighted, lax.ppermute(weighted, "core", swap), features)
    pieces = sum_over_tok(pieces, curve)

    kept = groups * across + 1
    keep, send, residual, rate = call(
        residual_kernel,
        "residual",
        [SCALAR] + [ON_CHIP] * 5,
        [tiles(kept), tiles(kept), pltpu.VMEM((classes, width), f32), tiles()],
        [pltpu.VMEM((2 * classes, width), bf16)],
    )(core, pieces, norm_now, right_side, high, low)
    pieces = sum_over_feat(keep, send)
    weighted, numbers = call(
        second_kernel, "second", [ON_CHIP] * 5, [tiles(groups * across + 1), tiles(3)]
    )(pieces, probability, scaled, first, norm_now)
    pieces, curve = call(
        functools.partial(image_kernel, step), "image", [SCALAR] + [ON_CHIP] * 4, image_outs, [put]
    )(core, weighted, lax.ppermute(weighted, "core", swap), high, low)
    pieces = sum_over_tok(pieces, curve)
    out = jax.ShapeDtypeStruct((classes, width), f32)
    return tuple(
        call(last_kernel, "last", [ON_CHIP] * 5, [out, out])(pieces, numbers, rate, right_side, residual)
    )


def solution(mesh):
    toks, feats = mesh.devices.shape
    across = math.isqrt(feats // 2)
    split = Mesh(mesh.devices.reshape(toks, across, across, 2), ("tok", "x", "y", "core"))
    feat = ("x", "y", "core")
    return jax.shard_map(
        on_device,
        mesh=split,
        in_specs=(P("tok", feat), P("tok"), P(None, feat), P(None, feat)),
        out_specs=(P(None, feat), P(None, feat)),
        check_vma=False,
    )
```

```python
import functools
import math

import jax
import jax.numpy as jnp
from jax import lax
from jax.experimental import pallas as pl
from jax.experimental.pallas import tpu as pltpu
from jax.sharding import Mesh, PartitionSpec as P

ridge_strength = 0.25
SUB, LANE = 8, 128
f32, bf16 = jnp.float32, jnp.bfloat16
ROWS_WITH_ROWS = (((1,), (1,)), ((), ()))
ROWS_WITH_COLUMNS = (((1,), (0,)), ((), ()))
ON_CHIP = pl.BlockSpec(memory_space=pltpu.VMEM)
SCALAR = pl.BlockSpec(memory_space=pltpu.SMEM)
IN_HBM = pl.BlockSpec(memory_space=pltpu.HBM)


def call(kernel, name, in_specs, outs, scratch=(), mib=8, kib=0, cost=None):
    return pl.pallas_call(
        kernel,
        out_shape=outs,
        in_specs=in_specs,
        out_specs=jax.tree.map(lambda _: ON_CHIP, outs),
        scratch_shapes=list(scratch),
        compiler_params=pltpu.CompilerParams(vmem_limit_bytes=kib << 10 if kib else mib << 20),
        cost_estimate=cost,
        name=name,
    )


def tiles(*lead):
    return pltpu.VMEM(lead + (SUB, LANE), f32)


def parts(x):
    high = x.astype(bf16)
    return high, (x - high.astype(f32)).astype(bf16)


def total(tile):
    return jnp.sum(tile, axis=(0, 1), keepdims=True)


def class_sum(pair):
    return jnp.sum(pair[0] + pair[1], axis=0, keepdims=True)


def fold(array):
    rows, columns = array.shape
    kept = None
    for r in range(rows // SUB):
        for c in range(columns // LANE):
            tile = array[r * SUB : (r + 1) * SUB, c * LANE : (c + 1) * LANE]
            kept = tile if kept is None else kept + tile
    return kept


def store_tiles(ref, value, extra):
    rows, columns = value.shape
    across = columns // LANE
    for r in range(rows // SUB):
        for c in range(across):
            ref[r * across + c] = value[r * SUB : (r + 1) * SUB, c * LANE : (c + 1) * LANE]
    ref[(rows // SUB) * across] = extra


def summed(pieces_ref, k):
    tile = pieces_ref[0, k]
    for i in range(1, pieces_ref.shape[0]):
        tile += pieces_ref[i, k]
    return tile


def prepare_kernel(
    labels_hbm, weights_hbm, right_hbm, count_ref, norm_ref, left_ref, labels_ref, weights_ref, right_ref, sems
):
    pairs = ((labels_hbm, labels_ref), (weights_hbm, weights_ref), (right_hbm, right_ref))
    copies = [pltpu.make_async_copy(*pair, sems.at[i]) for i, pair in enumerate(pairs)]
    for copy in copies:
        copy.start()
    copies[0].wait()
    ids = lax.broadcasted_iota(jnp.int32, (SUB, LANE), 0)
    for r in range(count_ref.shape[0]):
        count = jnp.zeros((SUB, LANE), f32)
        for row in range(labels_ref.shape[0]):
            count += (labels_ref[row : row + 1, :] == ids + r * SUB).astype(f32)
        count_ref[r] = count
    classes = weights_ref.shape[0]
    rows = 2 * classes
    for i, ref in enumerate((weights_ref, right_ref)):
        copies[i + 1].wait()
        high, low = parts(ref[...])
        left_ref[i * classes : (i + 1) * classes] = high
        left_ref[rows + i * classes : rows + (i + 1) * classes] = low
    right = right_ref[...]
    norm_ref[...] = fold(right * right)


def read_half(row, step, features_ref, block_ref, sems):
    half, width = features_ref.shape[0] // 2, features_ref.shape[1]
    rows = pl.ds(pl.multiple_of(row, half), half)
    copies = []
    for k in range(width // step):
        copies.append(
            pltpu.make_async_copy(features_ref.at[rows, pl.ds(k * step, step)], block_ref.at[k], sems.at[k])
        )
        copies[-1].start()
    return copies


def project_half(copies, step, left_ref, block_ref):
    rows, half = left_ref.shape[0] // 2, block_ref.shape[1]
    both = jnp.zeros((2 * rows, half), f32)
    rest = jnp.zeros((rows, half), f32)
    for k, copy in enumerate(copies):
        part = slice(k * step, (k + 1) * step)
        copy.wait()
        high, low = parts(block_ref[k])
        both += lax.dot_general(left_ref[:, part], high, ROWS_WITH_ROWS, preferred_element_type=f32)
        rest += lax.dot_general(left_ref[:rows, part], low, ROWS_WITH_ROWS, preferred_element_type=f32)
    return both[:rows] + both[rows:] + rest


def first_kernel(step, own, core_ref, left_ref, norm_ref, features_ref, out_ref, block_ref, sems):
    half = features_ref.shape[0] // 2
    which = core_ref[0] if own else 1 - core_ref[0]
    copies = read_half(which * half, step, features_ref, block_ref, sems)
    store_tiles(out_ref, project_half(copies, step, left_ref, block_ref), norm_ref[...])


def spread_kernel(keep_ref, got_ref, spread_ref):
    value = keep_ref[...] + got_ref[...]
    for i in range(spread_ref.shape[0]):
        spread_ref[i] = value


def spread_first_kernel(keep_ref, got_ref, count_ref, other_ref, spread_ref, counts_ref):
    spread_kernel(keep_ref, got_ref, spread_ref)
    for r in range(counts_ref.shape[0]):
        counts_ref[r] = count_ref[r] + other_ref[r]


def middle_kernel(pieces_ref, other_ref, sum_ref):
    count = pieces_ref.shape[1]
    for k in range(count):
        sum_ref[k] = summed(pieces_ref, k)
    for r in range(other_ref.shape[0]):
        sum_ref[count + r] = other_ref[r]


def keep_kernel(
    step,
    core_ref,
    features_ref,
    order_ref,
    high_own_ref,
    low_own_ref,
    high_other_ref,
    low_other_ref,
    done_ref,
    own_block_ref,
    other_block_ref,
    own_sems,
    other_sems,
):
    half = features_ref.shape[0] // 2
    core = core_ref[0]
    own = read_half(core * half, step, features_ref, own_block_ref, own_sems)
    other = read_half((1 - core) * half, step, features_ref, other_block_ref, other_sems)
    for copies, block_ref, high_ref, low_ref in (
        (own, own_block_ref, high_own_ref, low_own_ref),
        (other, other_block_ref, high_other_ref, low_other_ref),
    ):
        for k, copy in enumerate(copies):
            part = slice(k * step, (k + 1) * step)
            copy.wait()
            high_ref[:, part], low_ref[:, part] = parts(block_ref[k])
    done_ref[...] = order_ref[0]


def gather_kernel(pieces_ref, extra_ref, spread_ref):
    copies, count = pieces_ref.shape[:2]
    for k in range(count):
        tile = summed(pieces_ref, k)
        for i in range(copies):
            spread_ref[i, k] = tile
    for i in range(copies):
        spread_ref[i, count] = extra_ref[...]


def weigh(c, across, projected, probability, scaled, weighted_ref):
    average = class_sum([projected[r] * probability[r] for r in range(2)])
    curve = jnp.zeros((SUB, LANE), f32)
    for r in range(2):
        value = scaled[r] * (projected[r] - average)
        weighted_ref[r * across + c] = value
        curve += projected[r] * value
    return curve


def softmax_kernel(
    core_ref,
    labels_ref,
    order_ref,
    own_ref,
    one_ref,
    two_ref,
    three_ref,
    probability_ref,
    scaled_ref,
    first_ref,
    norm_ref,
    weighted_ref,
):
    def whole_sum(k):
        return own_ref[k] + one_ref[k] + two_ref[k] + three_ref[k]

    across = first_ref.shape[0] // 2
    classes = 2 * SUB
    ids = lax.broadcasted_iota(jnp.int32, (SUB, LANE), 0)
    counts = [jnp.sum(whole_sum(4 * across + 1 + r), axis=1, keepdims=True) for r in range(2)]
    curve = jnp.zeros((SUB, LANE), f32)
    for c in range(across):
        powered = [jnp.exp(whole_sum(r * across + c)) for r in range(2)]
        projected = [whole_sum((2 + r) * across + c) for r in range(2)]
        whole = class_sum(powered)
        probability = [powered[r] / whole for r in range(2)]
        label = labels_ref[pl.ds(core_ref[0] * across + c, 1), :]
        own = class_sum([jnp.where(label == ids + r * SUB, counts[r], 0.0) for r in range(2)])
        scale = 1.0 / (classes * own)
        scaled = [scale * probability[r] for r in range(2)]
        for r in range(2):
            probability_ref[r * across + c] = probability[r]
            scaled_ref[r * across + c] = scaled[r]
            first_ref[r * across + c] = projected[r]
        curve += weigh(c, across, projected, probability, scaled, weighted_ref)
    weighted_ref[2 * across] = curve
    norm_ref[...] = jnp.broadcast_to(total(whole_sum(4 * across)), (SUB, LANE))


def second_kernel(pieces_ref, probability_ref, scaled_ref, first_ref, norm_ref, weighted_ref, numbers_ref):
    across = first_ref.shape[0] // 2
    sums = summed(pieces_ref, 2 * across)
    norm_next, cross = total(sums[:4]), total(sums[4:])
    norm_now = norm_ref[0:1, 0:1]
    ratio = norm_next / norm_now
    curve = jnp.zeros((SUB, LANE), f32)
    for c in range(across):
        projected, probability, scaled = [], [], []
        for r in range(2):
            i = r * across + c
            projected.append(summed(pieces_ref, i) + ratio * first_ref[i])
            probability.append(probability_ref[i])
            scaled.append(scaled_ref[i])
        curve += weigh(c, across, projected, probability, scaled, weighted_ref)
    weighted_ref[2 * across] = curve
    norm_direction = norm_next + ratio * (2.0 * cross + ratio * norm_now)
    for i, value in enumerate((norm_next, ratio, norm_direction)):
        numbers_ref[i] = jnp.broadcast_to(value, (SUB, LANE))


def put_together(weighted_ref, left_ref):
    across = (weighted_ref.shape[0] - 1) // 2
    classes = 2 * SUB
    for r in range(2):
        for c in range(across):
            high, low = parts(weighted_ref[r * across + c])
            at = slice(c * LANE, (c + 1) * LANE)
            left_ref[r * SUB : (r + 1) * SUB, at] = high.astype(f32)
            left_ref[classes + r * SUB : classes + (r + 1) * SUB, at] = low.astype(f32)
    return left_ref[...].astype(bf16)


def image_columns(k, step, left, high_ref, low_ref, before_ref, pieces_ref):
    classes = left.shape[0] // 2
    share = pieces_ref.shape[1] // 2
    per = share * LANE
    part = slice(k * step, (k + 1) * step)
    both = lax.dot_general(left, high_ref[:, part], ROWS_WITH_COLUMNS, preferred_element_type=f32)
    rest = lax.dot_general(left[:classes], low_ref[:, part], ROWS_WITH_COLUMNS, preferred_element_type=f32)
    value = both[:classes] + both[classes:] + rest
    for z in range(step // per):
        for r in range(2):
            for c in range(share):
                at = z * per + c * LANE
                tile = value[r * SUB : (r + 1) * SUB, at : at + LANE]
                to = k * (step // per) + z
                if before_ref is not None:
                    tile = tile + before_ref[to, r * share + c]
                pieces_ref[to, r * share + c] = tile


def image_kernel(step, weighted_ref, high_ref, low_ref, before_ref, pieces_ref, left_ref):
    left = put_together(weighted_ref, left_ref)
    for k in range(high_ref.shape[1] // step):
        image_columns(k, step, left, high_ref, low_ref, before_ref, pieces_ref)


def image_own_kernel(step, weighted_ref, high_ref, low_ref, pieces_ref, left_ref):
    image_kernel(step, weighted_ref, high_ref, low_ref, None, pieces_ref, left_ref)


def image_other_kernel(
    step, other_ref, own_ref, high_ref, low_ref, before_ref, pieces_ref, curve_ref, left_ref
):
    last = own_ref.shape[0] - 1
    curve_ref[...] = own_ref[last] + other_ref[last]
    image_kernel(step, other_ref, high_ref, low_ref, before_ref, pieces_ref, left_ref)


def columns_of(pieces_ref, z, share, classes):
    rows = []
    for r in range(classes // SUB):
        rows.append(jnp.concatenate([pieces_ref[z, r * share + c] for c in range(share)], axis=1))
    return jnp.concatenate(rows, axis=0)


def project_kept(left_ref, high_ref, low_ref):
    classes = left_ref.shape[0] // 2
    left = left_ref[...]
    both = lax.dot_general(left, high_ref[...], ROWS_WITH_ROWS, preferred_element_type=f32)
    rest = lax.dot_general(left[:classes], low_ref[...], ROWS_WITH_ROWS, preferred_element_type=f32)
    return both[:classes] + both[classes:] + rest


def residual_other_kernel(
    pieces_ref, norm_ref, right_ref, high_ref, low_ref, send_ref, residual_ref, rate_ref, left_ref
):
    classes, width = right_ref.shape
    toks, count = pieces_ref.shape[:2]
    share = (count - 1) // 2
    per = share * LANE
    norm_now = norm_ref[0:1, 0:1]
    curve = total(summed(pieces_ref, count - 1))
    rate = norm_now / (curve + ridge_strength * norm_now)
    rate_ref[...] = jnp.broadcast_to(rate, (SUB, LANE))
    norm = jnp.zeros((SUB, LANE), f32)
    cross = jnp.zeros((SUB, LANE), f32)
    for z in range(toks):
        at = slice(z * per, (z + 1) * per)
        right = right_ref[:, at]
        residual = right - rate * (columns_of(pieces_ref, z, share, classes) + ridge_strength * right)
        residual_ref[:, at] = residual
        norm += fold(residual * residual)
        cross += fold(residual * right)
        high, low = parts(residual)
        left_ref[:classes, at] = high
        left_ref[classes:, at] = low
    sums = jnp.concatenate([norm[:4] + norm[4:], cross[:4] + cross[4:]])
    store_tiles(send_ref, project_kept(left_ref, high_ref, low_ref), sums)


def residual_own_kernel(left_ref, high_ref, low_ref, send_ref, keep_ref):
    store_tiles(keep_ref, project_kept(left_ref, high_ref, low_ref), send_ref[send_ref.shape[0] - 1])


def last_kernel(pieces_ref, numbers_ref, rate_ref, right_ref, old_ref, solution_ref, residual_ref):
    classes, width = right_ref.shape
    toks, count = pieces_ref.shape[:2]
    share = (count - 1) // 2
    per = share * LANE
    norm_next, ratio, norm_direction = [numbers_ref[i, 0:1, 0:1] for i in range(3)]
    curve = total(summed(pieces_ref, count - 1))
    rate = norm_next / (curve + ridge_strength * norm_direction)
    rate_first = rate_ref[0:1, 0:1]
    for z in range(toks):
        at = slice(z * per, (z + 1) * per)
        right, old = right_ref[:, at], old_ref[:, at]
        direction = old + ratio * right
        image = columns_of(pieces_ref, z, share, classes) + ridge_strength * direction
        solution_ref[:, at] = rate_first * right + rate * direction
        residual_ref[:, at] = old - rate * image


def on_device(features, labels, weights, right_side):
    classes, width = weights.shape
    tokens = features.shape[0]
    half = tokens // 2
    across = half // LANE
    groups = classes // SUB
    toks = lax.axis_size("tok")
    across_x, across_y = lax.axis_size("x"), lax.axis_size("y")
    share = width // toks // LANE
    core = lax.axis_index("core").astype(jnp.int32).reshape(1)
    labels = labels.reshape(tokens // LANE, LANE)
    step = min(512, width)
    swap = [(0, 1), (1, 0)]
    half_product = pl.CostEstimate(
        flops=12 * classes * half * width, bytes_accessed=4 * half * width, transcendentals=0
    )
    reading = [pltpu.VMEM((width // step, half, step), f32), pltpu.SemaphoreType.DMA((width // step,))]
    short = pl.CostEstimate(flops=0, bytes_accessed=1024, transcendentals=0)
    kept_half = pltpu.VMEM((half, width), bf16)
    image_outs = tiles(toks, groups * share)
    put = pltpu.VMEM((2 * classes, half), f32)

    def with_step(kernel):
        return functools.partial(kernel, step)

    def swapped(value):
        return lax.ppermute(value, "core", swap)

    def from_tok(value, distances):
        pairs = [
            ((z + distances[y]) % toks * across_y + y, z * across_y + y)
            for z in range(toks)
            for y in range(across_y)
        ]
        return lax.ppermute(value, ("tok", "y"), pairs)

    def sum_over_tok(pieces, curve):
        pieces = lax.all_to_all(pieces, "tok", 0, 0)
        spread = call(gather_kernel, "gather", [ON_CHIP] * 2, tiles(toks, groups * share + 1))(pieces, curve)
        return lax.all_to_all(spread, "tok", 0, 0)

    near, far = (-1, 2, 2, -1), (0, 1, 2, -2)
    count, norm, left = call(
        prepare_kernel,
        "prepare",
        [IN_HBM] * 3,
        [tiles(groups), tiles(), pltpu.VMEM((4 * classes, width), bf16)],
        [
            pltpu.VMEM(labels.shape, labels.dtype),
            pltpu.VMEM((classes, width), f32),
            pltpu.VMEM((classes, width), f32),
            pltpu.SemaphoreType.DMA((3,)),
        ],
        kib=61700,
    )(labels, weights, right_side)
    other = from_tok(count, near)
    kept = 2 * groups * across + 1

    def first_half(own, name):
        return call(
            functools.partial(first_kernel, step, own),
            name,
            [SCALAR, ON_CHIP, ON_CHIP, IN_HBM],
            tiles(kept),
            reading,
            mib=53,
            cost=short,
        )(core, left, norm, features)

    got = swapped(first_half(False, "first_other"))
    keep = first_half(True, "first_own")
    spread, count = call(
        spread_first_kernel, "spread_x", [ON_CHIP] * 4, [tiles(across_x, kept), tiles(groups)]
    )(keep, got, count, other)
    other = from_tok(count, far)
    pieces = lax.all_to_all(spread, "x", 0, 0)
    own = call(middle_kernel, "middle", [ON_CHIP] * 2, tiles(kept + groups))(pieces, other)
    others = [
        lax.ppermute(own, "y", [(i, (i + d) % across_y) for i in range(across_y)]) for d in range(1, across_y)
    ]
    high_own, low_own, high_other, low_other, done = call(
        with_step(keep_kernel),
        "keep",
        [SCALAR, IN_HBM, ON_CHIP],
        [kept_half] * 4 + [tiles()],
        reading[:1] * 2 + reading[1:] * 2,
        mib=45,
        cost=pl.CostEstimate(flops=0, bytes_accessed=20 * half * width, transcendentals=0),
    )(core, features, own)
    probability, scaled, first, norm_now, weighted = call(
        softmax_kernel,
        "softmax",
        [SCALAR] + [ON_CHIP] * 6,
        [tiles(groups * across)] * 3 + [tiles(), tiles(groups * across + 1)],
    )(core, labels, done, own, *others)

    def image(weighted):
        other = swapped(weighted)
        pieces = call(
            with_step(image_own_kernel), "image_own", [ON_CHIP] * 3, image_outs, [put], cost=half_product
        )(weighted, high_own, low_own)
        return call(
            with_step(image_other_kernel), "image_other", [ON_CHIP] * 5, [image_outs, tiles()], [put]
        )(other, weighted, high_other, low_other, pieces)

    pieces = sum_over_tok(*image(weighted))

    kept = groups * across + 1
    send, residual, rate, left = call(
        residual_other_kernel,
        "residual_other",
        [ON_CHIP] * 5,
        [tiles(kept), pltpu.VMEM((classes, width), f32), tiles(), pltpu.VMEM((2 * classes, width), bf16)],
    )(pieces, norm_now, right_side, high_other, low_other)
    got = swapped(send)
    keep = call(residual_own_kernel, "residual_own", [ON_CHIP] * 4, tiles(kept), cost=half_product)(
        left, high_own, low_own, send
    )
    spread = call(spread_kernel, "spread", [ON_CHIP] * 2, tiles(across_x * across_y, kept))(keep, got)
    pieces = lax.all_to_all(spread, ("x", "y"), 0, 0)
    weighted, numbers = call(second_kernel, "second", [ON_CHIP] * 5, [tiles(kept), tiles(3)])(
        pieces, probability, scaled, first, norm_now
    )

    pieces = sum_over_tok(*image(weighted))
    out = jax.ShapeDtypeStruct((classes, width), f32)
    return tuple(
        call(last_kernel, "last", [ON_CHIP] * 5, [out, out])(pieces, numbers, rate, right_side, residual)
    )


def solution(mesh):
    toks, feats = mesh.devices.shape
    across = math.isqrt(feats // 2)
    split = Mesh(mesh.devices.reshape(toks, across, across, 2), ("tok", "x", "y", "core"))
    feat = ("x", "y", "core")
    return jax.shard_map(
        on_device,
        mesh=split,
        in_specs=(P("tok", feat), P("tok"), P(None, feat), P(None, feat)),
        out_specs=(P(None, feat), P(None, feat)),
        check_vma=False,
    )
```

```python
import functools
import math

import jax
import jax.numpy as jnp
from jax import lax
from jax.experimental import pallas as pl
from jax.experimental.pallas import tpu as pltpu
from jax.sharding import Mesh, PartitionSpec as P

ridge_strength = 0.25
SUB, LANE = 8, 128
f32, bf16 = jnp.float32, jnp.bfloat16
ROWS_WITH_ROWS = (((1,), (1,)), ((), ()))
ROWS_WITH_COLUMNS = (((1,), (0,)), ((), ()))
ON_CHIP = pl.BlockSpec(memory_space=pltpu.VMEM)
SCALAR = pl.BlockSpec(memory_space=pltpu.SMEM)
IN_HBM = pl.BlockSpec(memory_space=pltpu.HBM)


def call(kernel, name, in_specs, outs, scratch=(), mib=8, kib=0, cost=None):
    return pl.pallas_call(
        kernel,
        out_shape=outs,
        in_specs=in_specs,
        out_specs=jax.tree.map(lambda _: ON_CHIP, outs),
        scratch_shapes=list(scratch),
        compiler_params=pltpu.CompilerParams(vmem_limit_bytes=kib << 10 if kib else mib << 20),
        cost_estimate=cost,
        name=name,
    )


def tiles(*lead):
    return pltpu.VMEM(lead + (SUB, LANE), f32)


def parts(x):
    high = x.astype(bf16)
    return high, (x - high.astype(f32)).astype(bf16)


def total(tile):
    return jnp.sum(tile, axis=(0, 1), keepdims=True)


def class_sum(pair):
    return jnp.sum(pair[0] + pair[1], axis=0, keepdims=True)


def fold(array):
    rows, columns = array.shape
    kept = None
    for r in range(rows // SUB):
        for c in range(columns // LANE):
            tile = array[r * SUB : (r + 1) * SUB, c * LANE : (c + 1) * LANE]
            kept = tile if kept is None else kept + tile
    return kept


def store_tiles(ref, value, extra):
    rows, columns = value.shape
    across = columns // LANE
    for r in range(rows // SUB):
        for c in range(across):
            ref[r * across + c] = value[r * SUB : (r + 1) * SUB, c * LANE : (c + 1) * LANE]
    ref[(rows // SUB) * across] = extra


def summed(pieces_ref, k):
    tile = pieces_ref[0, k]
    for i in range(1, pieces_ref.shape[0]):
        tile += pieces_ref[i, k]
    return tile


def read_half(row, step, features_ref, block_ref, sems):
    half, width = features_ref.shape[0] // 2, features_ref.shape[1]
    rows = pl.ds(pl.multiple_of(row, half), half)
    copies = []
    for k in range(width // step):
        copies.append(
            pltpu.make_async_copy(features_ref.at[rows, pl.ds(k * step, step)], block_ref.at[k], sems.at[k])
        )
        copies[-1].start()
    return copies


def project_half(copies, step, left_ref, block_ref, high_ref, low_ref):
    rows, half = left_ref.shape[0] // 2, block_ref.shape[1]
    both = jnp.zeros((2 * rows, half), f32)
    rest = jnp.zeros((rows, half), f32)
    for k, copy in enumerate(copies):
        part = slice(k * step, (k + 1) * step)
        copy.wait()
        high_ref[:, part], low_ref[:, part] = parts(block_ref[k])
        both += lax.dot_general(left_ref[:, part], high_ref[:, part], ROWS_WITH_ROWS, preferred_element_type=f32)
        rest += lax.dot_general(left_ref[:rows, part], low_ref[:, part], ROWS_WITH_ROWS, preferred_element_type=f32)
    return both[:rows] + both[rows:] + rest


def first_other_kernel(
    step,
    core_ref,
    labels_hbm,
    weights_hbm,
    right_hbm,
    features_ref,
    send_ref,
    count_ref,
    left_ref,
    high_ref,
    low_ref,
    labels_ref,
    weights_ref,
    right_ref,
    block_ref,
    sems,
    block_sems,
):
    pairs = ((weights_hbm, weights_ref), (right_hbm, right_ref), (labels_hbm, labels_ref))
    loads = [pltpu.make_async_copy(*pair, sems.at[i]) for i, pair in enumerate(pairs)]
    for load in loads:
        load.start()
    half = features_ref.shape[0] // 2
    copies = read_half((1 - core_ref[0]) * half, step, features_ref, block_ref, block_sems)
    classes = weights_ref.shape[0]
    rows = 2 * classes
    for i, ref in enumerate((weights_ref, right_ref)):
        loads[i].wait()
        high, low = parts(ref[...])
        left_ref[i * classes : (i + 1) * classes] = high
        left_ref[rows + i * classes : rows + (i + 1) * classes] = low
    right = right_ref[...]
    norm = fold(right * right)
    loads[2].wait()
    ids = lax.broadcasted_iota(jnp.int32, (SUB, LANE), 0)
    for r in range(count_ref.shape[0]):
        count = jnp.zeros((SUB, LANE), f32)
        for row in range(labels_ref.shape[0]):
            count += (labels_ref[row : row + 1, :] == ids + r * SUB).astype(f32)
        count_ref[r] = count
    store_tiles(send_ref, project_half(copies, step, left_ref, block_ref, high_ref, low_ref), norm)


def first_own_kernel(
    step, core_ref, left_ref, send_ref, features_ref, keep_ref, high_ref, low_ref, block_ref, sems
):
    half = features_ref.shape[0] // 2
    copies = read_half(core_ref[0] * half, step, features_ref, block_ref, sems)
    store_tiles(keep_ref, project_half(copies, step, left_ref, block_ref, high_ref, low_ref), send_ref[send_ref.shape[0] - 1])


def add_kernel(*refs):
    value = refs[0][...]
    for ref in refs[1:-1]:
        value += ref[...]
    refs[-1][...] = value


def join_kernel(keep_ref, got_ref, count_ref, other_ref, sum_ref, counts_ref):
    sum_ref[...] = keep_ref[...] + got_ref[...]
    counts_ref[...] = count_ref[...] + other_ref[...]


def middle_kernel(own_ref, one_ref, two_ref, three_ref, other_ref, sum_ref):
    count = own_ref.shape[0]
    for k in range(count):
        sum_ref[k] = own_ref[k] + one_ref[k] + two_ref[k] + three_ref[k]
    for r in range(other_ref.shape[0]):
        sum_ref[count + r] = other_ref[r]


def gather_kernel(pieces_ref, extra_ref, spread_ref):
    copies, count = pieces_ref.shape[:2]
    for k in range(count):
        tile = summed(pieces_ref, k)
        for i in range(copies):
            spread_ref[i, k] = tile
    for i in range(copies):
        spread_ref[i, count] = extra_ref[...]


def weigh(c, across, projected, probability, scaled, weighted_ref):
    average = class_sum([projected[r] * probability[r] for r in range(2)])
    curve = jnp.zeros((SUB, LANE), f32)
    for r in range(2):
        value = scaled[r] * (projected[r] - average)
        weighted_ref[r * across + c] = value
        curve += projected[r] * value
    return curve


def softmax_kernel(
    core_ref,
    labels_ref,
    own_ref,
    one_ref,
    two_ref,
    three_ref,
    probability_ref,
    scaled_ref,
    first_ref,
    norm_ref,
    weighted_ref,
):
    def whole_sum(k):
        return own_ref[k] + one_ref[k] + two_ref[k] + three_ref[k]

    across = first_ref.shape[0] // 2
    classes = 2 * SUB
    ids = lax.broadcasted_iota(jnp.int32, (SUB, LANE), 0)
    counts = [jnp.sum(whole_sum(4 * across + 1 + r), axis=1, keepdims=True) for r in range(2)]
    curve = jnp.zeros((SUB, LANE), f32)
    for c in range(across):
        powered = [jnp.exp(whole_sum(r * across + c)) for r in range(2)]
        projected = [whole_sum((2 + r) * across + c) for r in range(2)]
        whole = class_sum(powered)
        probability = [powered[r] / whole for r in range(2)]
        label = labels_ref[pl.ds(core_ref[0] * across + c, 1), :]
        own = class_sum([jnp.where(label == ids + r * SUB, counts[r], 0.0) for r in range(2)])
        scale = 1.0 / (classes * own)
        scaled = [scale * probability[r] for r in range(2)]
        for r in range(2):
            probability_ref[r * across + c] = probability[r]
            scaled_ref[r * across + c] = scaled[r]
            first_ref[r * across + c] = projected[r]
        curve += weigh(c, across, projected, probability, scaled, weighted_ref)
    weighted_ref[2 * across] = curve
    norm_ref[...] = jnp.broadcast_to(total(whole_sum(4 * across)), (SUB, LANE))


def second_kernel(pieces_ref, probability_ref, scaled_ref, first_ref, norm_ref, weighted_ref, numbers_ref):
    across = first_ref.shape[0] // 2
    sums = summed(pieces_ref, 2 * across)
    norm_next, cross = total(sums[:4]), total(sums[4:])
    norm_now = norm_ref[0:1, 0:1]
    ratio = norm_next / norm_now
    curve = jnp.zeros((SUB, LANE), f32)
    for c in range(across):
        projected, probability, scaled = [], [], []
        for r in range(2):
            i = r * across + c
            projected.append(summed(pieces_ref, i) + ratio * first_ref[i])
            probability.append(probability_ref[i])
            scaled.append(scaled_ref[i])
        curve += weigh(c, across, projected, probability, scaled, weighted_ref)
    weighted_ref[2 * across] = curve
    norm_direction = norm_next + ratio * (2.0 * cross + ratio * norm_now)
    for i, value in enumerate((norm_next, ratio, norm_direction)):
        numbers_ref[i] = jnp.broadcast_to(value, (SUB, LANE))


def put_together(weighted_ref, left_ref):
    across = (weighted_ref.shape[0] - 1) // 2
    classes = 2 * SUB
    for r in range(2):
        for c in range(across):
            high, low = parts(weighted_ref[r * across + c])
            at = slice(c * LANE, (c + 1) * LANE)
            left_ref[r * SUB : (r + 1) * SUB, at] = high.astype(f32)
            left_ref[classes + r * SUB : classes + (r + 1) * SUB, at] = low.astype(f32)
    return left_ref[...].astype(bf16)


def image_columns(k, step, left, high_ref, low_ref, before_ref, pieces_ref):
    classes = left.shape[0] // 2
    share = pieces_ref.shape[1] // 2
    per = share * LANE
    part = slice(k * step, (k + 1) * step)
    both = lax.dot_general(left, high_ref[:, part], ROWS_WITH_COLUMNS, preferred_element_type=f32)
    rest = lax.dot_general(left[:classes], low_ref[:, part], ROWS_WITH_COLUMNS, preferred_element_type=f32)
    value = both[:classes] + both[classes:] + rest
    for z in range(step // per):
        for r in range(2):
            for c in range(share):
                at = z * per + c * LANE
                tile = value[r * SUB : (r + 1) * SUB, at : at + LANE]
                to = k * (step // per) + z
                if before_ref is not None:
                    tile = tile + before_ref[to, r * share + c]
                pieces_ref[to, r * share + c] = tile


def image_kernel(step, weighted_ref, high_ref, low_ref, before_ref, pieces_ref, left_ref):
    left = put_together(weighted_ref, left_ref)
    for k in range(high_ref.shape[1] // step):
        image_columns(k, step, left, high_ref, low_ref, before_ref, pieces_ref)


def image_own_kernel(step, weighted_ref, high_ref, low_ref, pieces_ref, left_ref):
    image_kernel(step, weighted_ref, high_ref, low_ref, None, pieces_ref, left_ref)


def image_other_kernel(
    step, other_ref, own_ref, high_ref, low_ref, before_ref, pieces_ref, curve_ref, left_ref
):
    last = own_ref.shape[0] - 1
    curve_ref[...] = own_ref[last] + other_ref[last]
    image_kernel(step, other_ref, high_ref, low_ref, before_ref, pieces_ref, left_ref)


def columns_of(pieces_ref, z, share, classes):
    rows = []
    for r in range(classes // SUB):
        rows.append(jnp.concatenate([pieces_ref[z, r * share + c] for c in range(share)], axis=1))
    return jnp.concatenate(rows, axis=0)


def project_kept(left_ref, high_ref, low_ref):
    classes = left_ref.shape[0] // 2
    left = left_ref[...]
    both = lax.dot_general(left, high_ref[...], ROWS_WITH_ROWS, preferred_element_type=f32)
    rest = lax.dot_general(left[:classes], low_ref[...], ROWS_WITH_ROWS, preferred_element_type=f32)
    return both[:classes] + both[classes:] + rest


def residual_other_kernel(
    pieces_ref, norm_ref, right_ref, high_ref, low_ref, send_ref, residual_ref, rate_ref, left_ref
):
    classes, width = right_ref.shape
    toks, count = pieces_ref.shape[:2]
    share = (count - 1) // 2
    per = share * LANE
    norm_now = norm_ref[0:1, 0:1]
    curve = total(summed(pieces_ref, count - 1))
    rate = norm_now / (curve + ridge_strength * norm_now)
    rate_ref[...] = jnp.broadcast_to(rate, (SUB, LANE))
    norm = jnp.zeros((SUB, LANE), f32)
    cross = jnp.zeros((SUB, LANE), f32)
    for z in range(toks):
        at = slice(z * per, (z + 1) * per)
        right = right_ref[:, at]
        residual = right - rate * (columns_of(pieces_ref, z, share, classes) + ridge_strength * right)
        residual_ref[:, at] = residual
        norm += fold(residual * residual)
        cross += fold(residual * right)
        high, low = parts(residual)
        left_ref[:classes, at] = high
        left_ref[classes:, at] = low
    sums = jnp.concatenate([norm[:4] + norm[4:], cross[:4] + cross[4:]])
    store_tiles(send_ref, project_kept(left_ref, high_ref, low_ref), sums)


def residual_own_kernel(left_ref, high_ref, low_ref, send_ref, keep_ref):
    store_tiles(keep_ref, project_kept(left_ref, high_ref, low_ref), send_ref[send_ref.shape[0] - 1])


def last_kernel(pieces_ref, numbers_ref, rate_ref, right_ref, old_ref, solution_ref, residual_ref):
    classes, width = right_ref.shape
    toks, count = pieces_ref.shape[:2]
    share = (count - 1) // 2
    per = share * LANE
    norm_next, ratio, norm_direction = [numbers_ref[i, 0:1, 0:1] for i in range(3)]
    curve = total(summed(pieces_ref, count - 1))
    rate = norm_next / (curve + ridge_strength * norm_direction)
    rate_first = rate_ref[0:1, 0:1]
    for z in range(toks):
        at = slice(z * per, (z + 1) * per)
        right, old = right_ref[:, at], old_ref[:, at]
        direction = old + ratio * right
        image = columns_of(pieces_ref, z, share, classes) + ridge_strength * direction
        solution_ref[:, at] = rate_first * right + rate * direction
        residual_ref[:, at] = old - rate * image


def on_device(features, labels, weights, right_side):
    classes, width = weights.shape
    tokens = features.shape[0]
    half = tokens // 2
    across = half // LANE
    groups = classes // SUB
    toks = lax.axis_size("tok")
    across_x, across_y = lax.axis_size("x"), lax.axis_size("y")
    share = width // toks // LANE
    core = lax.axis_index("core").astype(jnp.int32).reshape(1)
    labels = labels.reshape(tokens // LANE, LANE)
    step = min(512, width)
    swap = [(0, 1), (1, 0)]
    half_product = pl.CostEstimate(
        flops=12 * classes * half * width, bytes_accessed=4 * half * width, transcendentals=0
    )
    reading = [pltpu.VMEM((width // step, half, step), f32), pltpu.SemaphoreType.DMA((width // step,))]
    kept_half = pltpu.VMEM((half, width), bf16)
    image_outs = tiles(toks, groups * share)
    put = pltpu.VMEM((2 * classes, half), f32)

    def with_step(kernel):
        return functools.partial(kernel, step)

    def swapped(value):
        return lax.ppermute(value, "core", swap)

    def from_tok(value, distances):
        pairs = [
            ((z + distances[y]) % toks * across_y + y, z * across_y + y)
            for z in range(toks)
            for y in range(across_y)
        ]
        return lax.ppermute(value, ("tok", "y"), pairs)

    def sum_over_tok(pieces, curve):
        pieces = lax.all_to_all(pieces, "tok", 0, 0)
        spread = call(gather_kernel, "gather", [ON_CHIP] * 2, tiles(toks, groups * share + 1))(pieces, curve)
        return lax.all_to_all(spread, "tok", 0, 0)

    near, far = (-1, 2, 2, -1), (0, 1, 2, -2)
    kept = 2 * groups * across + 1
    send, count, left, high_other, low_other = call(
        with_step(first_other_kernel),
        "first_other",
        [SCALAR] + [IN_HBM] * 4,
        [tiles(kept), tiles(groups), pltpu.VMEM((4 * classes, width), bf16), kept_half, kept_half],
        [
            pltpu.VMEM(labels.shape, labels.dtype),
            pltpu.VMEM((classes, width), f32),
            pltpu.VMEM((classes, width), f32),
            reading[0],
            pltpu.SemaphoreType.DMA((3,)),
            reading[1],
        ],
        kib=61560 - 4096,
    )(core, labels, weights, right_side, features)
    got = swapped(send)
    other = from_tok(count, near)
    keep, high_own, low_own = call(
        with_step(first_own_kernel),
        "first_own",
        [SCALAR, ON_CHIP, ON_CHIP, IN_HBM],
        [tiles(kept), kept_half, kept_half],
        reading,
        mib=45,
        cost=half_product,
    )(core, left, send, features)

    def from_others(value, axis, count):
        return [
            lax.ppermute(value, axis, [(i, (i + d) % count) for i in range(count)]) for d in range(1, count)
        ]

    own, count = call(join_kernel, "join", [ON_CHIP] * 4, [tiles(kept), tiles(groups)])(keep, got, count, other)
    others = from_others(own, "x", across_x)
    other = from_tok(count, far)
    own = call(middle_kernel, "middle", [ON_CHIP] * 5, tiles(kept + groups))(own, *others, other)
    others = from_others(own, "y", across_y)
    probability, scaled, first, norm_now, weighted = call(
        softmax_kernel,
        "softmax",
        [SCALAR] + [ON_CHIP] * 5,
        [tiles(groups * across)] * 3 + [tiles(), tiles(groups * across + 1)],
    )(core, labels, own, *others)

    def image(weighted):
        other = swapped(weighted)
        pieces = call(
            with_step(image_own_kernel), "image_own", [ON_CHIP] * 3, image_outs, [put], cost=half_product
        )(weighted, high_own, low_own)
        return call(
            with_step(image_other_kernel), "image_other", [ON_CHIP] * 5, [image_outs, tiles()], [put]
        )(other, weighted, high_other, low_other, pieces)

    pieces = sum_over_tok(*image(weighted))

    kept = groups * across + 1
    send, residual, rate, left = call(
        residual_other_kernel,
        "residual_other",
        [ON_CHIP] * 5,
        [tiles(kept), pltpu.VMEM((classes, width), f32), tiles(), pltpu.VMEM((2 * classes, width), bf16)],
    )(pieces, norm_now, right_side, high_other, low_other)
    got = swapped(send)
    keep = call(residual_own_kernel, "residual_own", [ON_CHIP] * 4, tiles(kept), cost=half_product)(
        left, high_own, low_own, send
    )
    own = call(add_kernel, "add", [ON_CHIP] * 2, tiles(kept))(keep, got)
    own = call(add_kernel, "add_x", [ON_CHIP] * 4, tiles(kept))(own, *from_others(own, "x", across_x))
    own = call(add_kernel, "add_y", [ON_CHIP] * 4, tiles(kept))(own, *from_others(own, "y", across_y))
    weighted, numbers = call(second_kernel, "second", [ON_CHIP] * 5, [tiles(kept), tiles(3)])(
        own[None], probability, scaled, first, norm_now
    )
    pieces = sum_over_tok(*image(weighted))
    out = jax.ShapeDtypeStruct((classes, width), f32)
    return tuple(
        call(last_kernel, "last", [ON_CHIP] * 5, [out, out])(pieces, numbers, rate, right_side, residual)
    )


def solution(mesh):
    toks, feats = mesh.devices.shape
    across = math.isqrt(feats // 2)
    split = Mesh(mesh.devices.reshape(toks, across, across, 2), ("tok", "x", "y", "core"))
    feat = ("x", "y", "core")
    return jax.shard_map(
        on_device,
        mesh=split,
        in_specs=(P("tok", feat), P("tok"), P(None, feat), P(None, feat)),
        out_specs=(P(None, feat), P(None, feat)),
        check_vma=False,
    )
```

```python
import functools
import math

import jax
import jax.numpy as jnp
from jax import lax
from jax.experimental import pallas as pl
from jax.experimental.pallas import tpu as pltpu
from jax.sharding import Mesh, PartitionSpec as P

ridge_strength = 0.25
SUB, LANE = 8, 128
f32, bf16 = jnp.float32, jnp.bfloat16
ROWS_WITH_ROWS = (((1,), (1,)), ((), ()))
ROWS_WITH_COLUMNS = (((1,), (0,)), ((), ()))
ON_CHIP = pl.BlockSpec(memory_space=pltpu.VMEM)
SCALAR = pl.BlockSpec(memory_space=pltpu.SMEM)
IN_HBM = pl.BlockSpec(memory_space=pltpu.HBM)


def call(kernel, name, in_specs, outs, scratch=(), mib=8, kib=0, cost=None):
    return pl.pallas_call(
        kernel,
        out_shape=outs,
        in_specs=in_specs,
        out_specs=jax.tree.map(lambda _: ON_CHIP, outs),
        scratch_shapes=list(scratch),
        compiler_params=pltpu.CompilerParams(vmem_limit_bytes=kib << 10 if kib else mib << 20),
        cost_estimate=cost,
        name=name,
    )


def tiles(*lead):
    return pltpu.VMEM(lead + (SUB, LANE), f32)


def parts(x):
    high = x.astype(bf16)
    return high, (x - high.astype(f32)).astype(bf16)


def total(tile):
    return jnp.sum(tile, axis=(0, 1), keepdims=True)


def class_sum(pair):
    return jnp.sum(pair[0] + pair[1], axis=0, keepdims=True)


def fold(array):
    rows, columns = array.shape
    kept = None
    for r in range(rows // SUB):
        for c in range(columns // LANE):
            tile = array[r * SUB : (r + 1) * SUB, c * LANE : (c + 1) * LANE]
            kept = tile if kept is None else kept + tile
    return kept


def store_tiles(ref, value, extra):
    rows, columns = value.shape
    across = columns // LANE
    for r in range(rows // SUB):
        for c in range(across):
            ref[r * across + c] = value[r * SUB : (r + 1) * SUB, c * LANE : (c + 1) * LANE]
    ref[(rows // SUB) * across] = extra


def summed(pieces_ref, k):
    tile = pieces_ref[0, k]
    for i in range(1, pieces_ref.shape[0]):
        tile += pieces_ref[i, k]
    return tile


def read_half(row, step, features_ref, block_ref, sems):
    half, width = features_ref.shape[0] // 2, features_ref.shape[1]
    rows = pl.ds(pl.multiple_of(row, half), half)
    copies = []
    for k in range(width // step):
        copies.append(
            pltpu.make_async_copy(features_ref.at[rows, pl.ds(k * step, step)], block_ref.at[k], sems.at[k])
        )
        copies[-1].start()
    return copies


def project_half(copies, step, left_ref, block_ref, high_ref, low_ref):
    rows, half = left_ref.shape[0] // 2, block_ref.shape[1]
    both = jnp.zeros((2 * rows, half), f32)
    rest = jnp.zeros((rows, half), f32)
    for k, copy in enumerate(copies):
        part = slice(k * step, (k + 1) * step)
        copy.wait()
        high_ref[:, part], low_ref[:, part] = parts(block_ref[k])
        both += lax.dot_general(left_ref[:, part], high_ref[:, part], ROWS_WITH_ROWS, preferred_element_type=f32)
        rest += lax.dot_general(left_ref[:rows, part], low_ref[:, part], ROWS_WITH_ROWS, preferred_element_type=f32)
    return both[:rows] + both[rows:] + rest


def first_other_kernel(
    step,
    place_ref,
    labels_hbm,
    weights_hbm,
    right_hbm,
    features_ref,
    send_ref,
    count_ref,
    left_ref,
    high_ref,
    low_ref,
    labels_ref,
    weights_ref,
    right_ref,
    block_ref,
    sems,
    block_sems,
):
    pairs = ((weights_hbm, weights_ref), (right_hbm, right_ref), (labels_hbm, labels_ref))
    loads = [pltpu.make_async_copy(*pair, sems.at[i]) for i, pair in enumerate(pairs)]
    for load in loads:
        load.start()
    half = features_ref.shape[0] // 2
    copies = read_half((1 - (place_ref[0] & 1)) * half, step, features_ref, block_ref, block_sems)
    classes = weights_ref.shape[0]
    rows = 2 * classes
    for i, ref in enumerate((weights_ref, right_ref)):
        loads[i].wait()
        high, low = parts(ref[...])
        left_ref[i * classes : (i + 1) * classes] = high
        left_ref[rows + i * classes : rows + (i + 1) * classes] = low
    right = right_ref[...]
    norm = fold(right * right)
    loads[2].wait()
    ids = lax.broadcasted_iota(jnp.int32, (SUB, LANE), 0)
    for r in range(count_ref.shape[0]):
        count = jnp.zeros((SUB, LANE), f32)
        for row in range(labels_ref.shape[0]):
            count += (labels_ref[row : row + 1, :] == ids + r * SUB).astype(f32)
        count_ref[r] = count
    store_tiles(send_ref, project_half(copies, step, left_ref, block_ref, high_ref, low_ref), norm)


def first_own_kernel(
    step, place_ref, left_ref, send_ref, features_ref, keep_ref, high_ref, low_ref, block_ref, sems
):
    half = features_ref.shape[0] // 2
    copies = read_half((place_ref[0] & 1) * half, step, features_ref, block_ref, sems)
    store_tiles(keep_ref, project_half(copies, step, left_ref, block_ref, high_ref, low_ref), send_ref[send_ref.shape[0] - 1])


def tree(values):
    while len(values) > 1:
        values = [values[i] + values[i + 1] for i in range(0, len(values), 2)]
    return values[0]


def add_kernel(*refs):
    refs[-1][...] = tree([ref[...] for ref in refs[:-1]])


def join_kernel(keep_ref, got_ref, count_ref, other_ref, sum_ref, counts_ref):
    sum_ref[...] = keep_ref[...] + got_ref[...]
    counts_ref[...] = count_ref[...] + other_ref[...]


def middle_kernel(own_ref, one_ref, two_ref, three_ref, other_ref, sum_ref):
    count = own_ref.shape[0]
    for k in range(count):
        sum_ref[k] = tree([own_ref[k], one_ref[k], two_ref[k], three_ref[k]])
    for r in range(other_ref.shape[0]):
        sum_ref[count + r] = other_ref[r]


def weigh(c, across, projected, probability, scaled, weighted_ref):
    average = class_sum([projected[r] * probability[r] for r in range(2)])
    curve = jnp.zeros((SUB, LANE), f32)
    for r in range(2):
        value = scaled[r] * (projected[r] - average)
        weighted_ref[r * across + c] = value
        curve += projected[r] * value
    return curve


def softmax_kernel(
    place_ref,
    labels_ref,
    own_ref,
    one_ref,
    two_ref,
    three_ref,
    probability_ref,
    scaled_ref,
    first_ref,
    norm_ref,
    weighted_ref,
):
    def whole_sum(k):
        return tree([own_ref[k], one_ref[k], two_ref[k], three_ref[k]])

    across = first_ref.shape[0] // 2
    classes = 2 * SUB
    ids = lax.broadcasted_iota(jnp.int32, (SUB, LANE), 0)
    counts = [jnp.sum(whole_sum(4 * across + 1 + r), axis=1, keepdims=True) for r in range(2)]
    curve = jnp.zeros((SUB, LANE), f32)
    for c in range(across):
        powered = [jnp.exp(whole_sum(r * across + c)) for r in range(2)]
        projected = [whole_sum((2 + r) * across + c) for r in range(2)]
        whole = class_sum(powered)
        probability = [powered[r] / whole for r in range(2)]
        label = labels_ref[pl.ds((place_ref[0] & 1) * across + c, 1), :]
        own = class_sum([jnp.where(label == ids + r * SUB, counts[r], 0.0) for r in range(2)])
        scale = 1.0 / (classes * own)
        scaled = [scale * probability[r] for r in range(2)]
        for r in range(2):
            probability_ref[r * across + c] = probability[r]
            scaled_ref[r * across + c] = scaled[r]
            first_ref[r * across + c] = projected[r]
        curve += weigh(c, across, projected, probability, scaled, weighted_ref)
    weighted_ref[2 * across] = curve
    norm_ref[...] = jnp.broadcast_to(total(whole_sum(4 * across)), (SUB, LANE))


def second_kernel(pieces_ref, probability_ref, scaled_ref, first_ref, norm_ref, weighted_ref, numbers_ref):
    across = first_ref.shape[0] // 2
    sums = summed(pieces_ref, 2 * across)
    norm_next, cross = total(sums[:4]), total(sums[4:])
    norm_now = norm_ref[0:1, 0:1]
    ratio = norm_next / norm_now
    curve = jnp.zeros((SUB, LANE), f32)
    for c in range(across):
        projected, probability, scaled = [], [], []
        for r in range(2):
            i = r * across + c
            projected.append(summed(pieces_ref, i) + ratio * first_ref[i])
            probability.append(probability_ref[i])
            scaled.append(scaled_ref[i])
        curve += weigh(c, across, projected, probability, scaled, weighted_ref)
    weighted_ref[2 * across] = curve
    norm_direction = norm_next + ratio * (2.0 * cross + ratio * norm_now)
    for i, value in enumerate((norm_next, ratio, norm_direction)):
        numbers_ref[i] = jnp.broadcast_to(value, (SUB, LANE))


def put_together(weighted_ref, left_ref):
    across = (weighted_ref.shape[0] - 1) // 2
    classes = 2 * SUB
    for r in range(2):
        for c in range(across):
            high, low = parts(weighted_ref[r * across + c])
            at = slice(c * LANE, (c + 1) * LANE)
            left_ref[r * SUB : (r + 1) * SUB, at] = high.astype(f32)
            left_ref[classes + r * SUB : classes + (r + 1) * SUB, at] = low.astype(f32)
    return left_ref[...].astype(bf16)


def image_columns(at, step, left, high_ref, low_ref):
    classes = left.shape[0] // 2
    part = pl.ds(at, step)
    both = lax.dot_general(left, high_ref[:, part], ROWS_WITH_COLUMNS, preferred_element_type=f32)
    rest = lax.dot_general(left[:classes], low_ref[:, part], ROWS_WITH_COLUMNS, preferred_element_type=f32)
    return both[:classes] + both[classes:] + rest


def image_own_kernel(step, weighted_ref, high_ref, low_ref, image_ref, left_ref):
    left = put_together(weighted_ref, left_ref)
    for k in range(high_ref.shape[1] // step):
        image_ref[k] = image_columns(k * step, step, left, high_ref, low_ref)


def image_other_kernel(
    step, place_ref, other_ref, own_ref, high_ref, low_ref, before_ref, *piece_refs_and_left
):
    *piece_refs, left_ref = piece_refs_and_left
    last = own_ref.shape[0] - 1
    curve = own_ref[last] + other_ref[last]
    left = put_together(other_ref, left_ref)
    for d, piece_ref in enumerate(piece_refs):
        block = (place_ref[0] >> 1) ^ d
        at = pl.multiple_of(block * step, step)
        store_tiles(piece_ref, before_ref[block] + image_columns(at, step, left, high_ref, low_ref), curve)


def columns_of(piece_ref, classes):
    across = (piece_ref.shape[0] - 1) // (classes // SUB)
    rows = []
    for r in range(classes // SUB):
        rows.append(jnp.concatenate([piece_ref[r * across + c] for c in range(across)], axis=1))
    return jnp.concatenate(rows, axis=0)


def project_kept(left_ref, high_ref, low_ref):
    classes = left_ref.shape[0] // 2
    left = left_ref[...]
    both = lax.dot_general(left, high_ref[...], ROWS_WITH_ROWS, preferred_element_type=f32)
    rest = lax.dot_general(left[:classes], low_ref[...], ROWS_WITH_ROWS, preferred_element_type=f32)
    return both[:classes] + both[classes:] + rest


def residual_other_kernel(
    step,
    place_ref,
    own_ref,
    one_ref,
    two_ref,
    three_ref,
    norm_ref,
    right_ref,
    high_ref,
    low_ref,
    send_ref,
    residual_ref,
    rate_ref,
    left_ref,
):
    classes = right_ref.shape[0]
    norm_now = norm_ref[0:1, 0:1]
    curve = total(own_ref[own_ref.shape[0] - 1])
    rate = norm_now / (curve + ridge_strength * norm_now)
    rate_ref[...] = jnp.broadcast_to(rate, (SUB, LANE))
    for d, piece_ref in enumerate((own_ref, one_ref, two_ref, three_ref)):
        at = pl.ds(pl.multiple_of(((place_ref[0] >> 1) ^ d) * step, step), step)
        right = right_ref[:, at]
        residual = right - rate * (columns_of(piece_ref, classes) + ridge_strength * right)
        residual_ref[:, at] = residual
        high, low = parts(residual)
        left_ref[:classes, at] = high
        left_ref[classes:, at] = low
    right, residual = right_ref[...], residual_ref[...]
    norm, cross = fold(residual * residual), fold(residual * right)
    sums = jnp.concatenate([norm[:4] + norm[4:], cross[:4] + cross[4:]])
    store_tiles(send_ref, project_kept(left_ref, high_ref, low_ref), sums)


def residual_own_kernel(left_ref, high_ref, low_ref, send_ref, keep_ref):
    store_tiles(keep_ref, project_kept(left_ref, high_ref, low_ref), send_ref[send_ref.shape[0] - 1])


def last_kernel(
    step,
    place_ref,
    own_ref,
    one_ref,
    two_ref,
    three_ref,
    numbers_ref,
    rate_ref,
    right_ref,
    old_ref,
    solution_ref,
    residual_ref,
):
    classes = right_ref.shape[0]
    norm_next, ratio, norm_direction = [numbers_ref[i, 0:1, 0:1] for i in range(3)]
    curve = total(own_ref[own_ref.shape[0] - 1])
    rate = norm_next / (curve + ridge_strength * norm_direction)
    rate_first = rate_ref[0:1, 0:1]
    for d, piece_ref in enumerate((own_ref, one_ref, two_ref, three_ref)):
        at = pl.ds(pl.multiple_of(((place_ref[0] >> 1) ^ d) * step, step), step)
        right, old = right_ref[:, at], old_ref[:, at]
        direction = old + ratio * right
        image = columns_of(piece_ref, classes) + ridge_strength * direction
        solution_ref[:, at] = rate_first * right + rate * direction
        residual_ref[:, at] = old - rate * image


def on_device(features, labels, weights, right_side):
    classes, width = weights.shape
    tokens = features.shape[0]
    half = tokens // 2
    across = half // LANE
    groups = classes // SUB
    toks = lax.axis_size("tok")
    across_x, across_y = lax.axis_size("x"), lax.axis_size("y")
    labels = labels.reshape(tokens // LANE, LANE)
    step = width // 4
    tok = lax.axis_index("tok").astype(jnp.int32)
    role = jnp.minimum(tok, toks - 1 - tok)
    place = (2 * role + lax.axis_index("core").astype(jnp.int32)).reshape(1)
    swap = [(0, 1), (1, 0)]
    half_product = pl.CostEstimate(
        flops=12 * classes * half * width, bytes_accessed=4 * half * width, transcendentals=0
    )
    reading = [pltpu.VMEM((width // step, half, step), f32), pltpu.SemaphoreType.DMA((width // step,))]
    kept_half = pltpu.VMEM((half, width), bf16)
    piece = tiles(groups * step // LANE + 1)
    put = pltpu.VMEM((2 * classes, half), f32)

    def with_step(kernel):
        return functools.partial(kernel, step)

    def swapped(value):
        return lax.ppermute(value, "core", swap)

    def from_tok(value, distances):
        pairs = [
            ((z + distances[y]) % toks * across_y + y, z * across_y + y)
            for z in range(toks)
            for y in range(across_y)
        ]
        return lax.ppermute(value, ("tok", "y"), pairs)

    def from_others(value, axis):
        values = value if isinstance(value, list) else [value] * 3
        count = lax.axis_size(axis)
        return [lax.ppermute(v, axis, [(i, i ^ (d + 1)) for i in range(count)]) for d, v in enumerate(values)]

    def add(name, *values):
        return call(add_kernel, name, [ON_CHIP] * len(values), tiles(values[0].shape[0]))(*values)

    def sum_over_tok(own, *rest):
        own = add("add_half", own, *from_others(list(rest), "tok"))
        own = add("add_tok", own, lax.ppermute(own, "tok", [(i, toks - 1 - i) for i in range(toks)]))
        return [own] + from_others(own, "tok")

    near, far = (-1, 2, 2, -1), (0, 1, 2, -2)
    kept = 2 * groups * across + 1
    send, count, left, high_other, low_other = call(
        with_step(first_other_kernel),
        "first_other",
        [SCALAR] + [IN_HBM] * 4,
        [tiles(kept), tiles(groups), pltpu.VMEM((4 * classes, width), bf16), kept_half, kept_half],
        [
            pltpu.VMEM(labels.shape, labels.dtype),
            pltpu.VMEM((classes, width), f32),
            pltpu.VMEM((classes, width), f32),
            reading[0],
            pltpu.SemaphoreType.DMA((3,)),
            reading[1],
        ],
        kib=61560 - 4096,
    )(place, labels, weights, right_side, features)
    got = swapped(send)
    other = from_tok(count, near)
    keep, high_own, low_own = call(
        with_step(first_own_kernel),
        "first_own",
        [SCALAR, ON_CHIP, ON_CHIP, IN_HBM],
        [tiles(kept), kept_half, kept_half],
        reading,
        mib=45,
        cost=half_product,
    )(place, left, send, features)

    own, count = call(join_kernel, "join", [ON_CHIP] * 4, [tiles(kept), tiles(groups)])(keep, got, count, other)
    others = from_others(own, "x")
    other = from_tok(count, far)
    own = call(middle_kernel, "middle", [ON_CHIP] * 5, tiles(kept + groups))(own, *others, other)
    others = from_others(own, "y")
    probability, scaled, first, norm_now, weighted = call(
        softmax_kernel,
        "softmax",
        [SCALAR] + [ON_CHIP] * 5,
        [tiles(groups * across)] * 3 + [tiles(), tiles(groups * across + 1)],
    )(place, labels, own, *others)

    def image(weighted):
        other = swapped(weighted)
        before = call(
            with_step(image_own_kernel),
            "image_own",
            [ON_CHIP] * 3,
            pltpu.VMEM((4, classes, step), f32),
            [put],
            cost=half_product,
        )(weighted, high_own, low_own)
        return call(
            with_step(image_other_kernel), "image_other", [SCALAR] + [ON_CHIP] * 5, [piece] * 4, [put]
        )(place, other, weighted, high_other, low_other, before)

    pieces = sum_over_tok(*image(weighted))

    kept = groups * across + 1
    send, residual, rate, left = call(
        with_step(residual_other_kernel),
        "residual_other",
        [SCALAR] + [ON_CHIP] * 8,
        [tiles(kept), pltpu.VMEM((classes, width), f32), tiles(), pltpu.VMEM((2 * classes, width), bf16)],
    )(place, *pieces, norm_now, right_side, high_other, low_other)
    got = swapped(send)
    keep = call(residual_own_kernel, "residual_own", [ON_CHIP] * 4, tiles(kept), cost=half_product)(
        left, high_own, low_own, send
    )
    own = add("add_core", keep, got)
    own = add("add_x", own, *from_others(own, "x"))
    own = add("add_y", own, *from_others(own, "y"))
    weighted, numbers = call(second_kernel, "second", [ON_CHIP] * 5, [tiles(kept), tiles(3)])(
        own[None], probability, scaled, first, norm_now
    )
    pieces = sum_over_tok(*image(weighted))
    out = jax.ShapeDtypeStruct((classes, width), f32)
    return tuple(
        call(with_step(last_kernel), "last", [SCALAR] + [ON_CHIP] * 8, [out, out])(
            place, *pieces, numbers, rate, right_side, residual
        )
    )


def solution(mesh):
    toks, feats = mesh.devices.shape
    across = math.isqrt(feats // 2)
    split = Mesh(mesh.devices.reshape(toks, across, across, 2), ("tok", "x", "y", "core"))
    feat = ("x", "y", "core")
    return jax.shard_map(
        on_device,
        mesh=split,
        in_specs=(P("tok", feat), P("tok"), P(None, feat), P(None, feat)),
        out_specs=(P(None, feat), P(None, feat)),
        check_vma=False,
    )
```

```python
import functools
import math

import jax
import jax.numpy as jnp
from jax import lax
from jax.experimental import pallas as pl
from jax.experimental.pallas import tpu as pltpu
from jax.sharding import Mesh, PartitionSpec as P

ridge_strength = 0.25
SUB, LANE = 8, 128
f32, bf16 = jnp.float32, jnp.bfloat16
ROWS_WITH_ROWS = (((1,), (1,)), ((), ()))
ROWS_WITH_COLUMNS = (((1,), (0,)), ((), ()))
ON_CHIP = pl.BlockSpec(memory_space=pltpu.VMEM)
SCALAR = pl.BlockSpec(memory_space=pltpu.SMEM)
IN_HBM = pl.BlockSpec(memory_space=pltpu.HBM)


def call(kernel, name, in_specs, outs, scratch=(), mib=8, kib=0, cost=None):
    return pl.pallas_call(
        kernel,
        out_shape=outs,
        in_specs=in_specs,
        out_specs=jax.tree.map(lambda _: ON_CHIP, outs),
        scratch_shapes=list(scratch),
        compiler_params=pltpu.CompilerParams(vmem_limit_bytes=kib << 10 if kib else mib << 20),
        cost_estimate=cost,
        name=name,
    )


def tiles(*lead):
    return pltpu.VMEM(lead + (SUB, LANE), f32)


def parts(x):
    high = x.astype(bf16)
    return high, (x - high.astype(f32)).astype(bf16)


def total(tile):
    return jnp.sum(tile, axis=(0, 1), keepdims=True)


def class_sum(pair):
    return jnp.sum(pair[0] + pair[1], axis=0, keepdims=True)


def fold(array):
    rows, columns = array.shape
    kept = None
    for r in range(rows // SUB):
        for c in range(columns // LANE):
            tile = array[r * SUB : (r + 1) * SUB, c * LANE : (c + 1) * LANE]
            kept = tile if kept is None else kept + tile
    return kept


def store_tiles(ref, value, extra):
    rows, columns = value.shape
    across = columns // LANE
    for r in range(rows // SUB):
        for c in range(across):
            ref[r * across + c] = value[r * SUB : (r + 1) * SUB, c * LANE : (c + 1) * LANE]
    ref[(rows // SUB) * across] = extra


def summed(pieces_ref, k):
    tile = pieces_ref[0, k]
    for i in range(1, pieces_ref.shape[0]):
        tile += pieces_ref[i, k]
    return tile


def read_half(row, step, features_ref, block_ref, sems):
    half, width = features_ref.shape[0] // 2, features_ref.shape[1]
    rows = pl.ds(pl.multiple_of(row, half), half)
    copies = []
    for k in range(width // step):
        copies.append(
            pltpu.make_async_copy(features_ref.at[rows, pl.ds(k * step, step)], block_ref.at[k], sems.at[k])
        )
        copies[-1].start()
    return copies


def project_half(copies, step, left_ref, block_ref, high_ref, low_ref):
    rows, half = left_ref.shape[0] // 2, block_ref.shape[1]
    both = jnp.zeros((2 * rows, half), f32)
    rest = jnp.zeros((rows, half), f32)
    for k, copy in enumerate(copies):
        part = slice(k * step, (k + 1) * step)
        copy.wait()
        high_ref[:, part], low_ref[:, part] = parts(block_ref[k])
        both += lax.dot_general(left_ref[:, part], high_ref[:, part], ROWS_WITH_ROWS, preferred_element_type=f32)
        rest += lax.dot_general(left_ref[:rows, part], low_ref[:, part], ROWS_WITH_ROWS, preferred_element_type=f32)
    return both[:rows] + both[rows:] + rest


def first_other_kernel(
    step,
    place_ref,
    labels_hbm,
    weights_hbm,
    right_hbm,
    features_ref,
    send_ref,
    count_ref,
    left_ref,
    high_ref,
    low_ref,
    labels_ref,
    weights_ref,
    right_ref,
    block_ref,
    sems,
    block_sems,
):
    pairs = ((weights_hbm, weights_ref), (right_hbm, right_ref), (labels_hbm, labels_ref))
    loads = [pltpu.make_async_copy(*pair, sems.at[i]) for i, pair in enumerate(pairs)]
    for load in loads:
        load.start()
    half = features_ref.shape[0] // 2
    copies = read_half((1 - (place_ref[0] & 1)) * half, step, features_ref, block_ref, block_sems)
    classes = weights_ref.shape[0]
    rows = 2 * classes
    for i, ref in enumerate((weights_ref, right_ref)):
        loads[i].wait()
        high, low = parts(ref[...])
        left_ref[i * classes : (i + 1) * classes] = high
        left_ref[rows + i * classes : rows + (i + 1) * classes] = low
    right = right_ref[...]
    norm = fold(right * right)
    loads[2].wait()
    ids = lax.broadcasted_iota(jnp.int32, (SUB, LANE), 0)
    for r in range(count_ref.shape[0]):
        count = jnp.zeros((SUB, LANE), f32)
        for row in range(labels_ref.shape[0]):
            count += (labels_ref[row : row + 1, :] == ids + r * SUB).astype(f32)
        count_ref[r] = count
    store_tiles(send_ref, project_half(copies, step, left_ref, block_ref, high_ref, low_ref), norm)


def first_own_kernel(
    step, place_ref, left_ref, send_ref, features_ref, keep_ref, high_ref, low_ref, block_ref, sems
):
    half = features_ref.shape[0] // 2
    copies = read_half((place_ref[0] & 1) * half, step, features_ref, block_ref, sems)
    store_tiles(keep_ref, project_half(copies, step, left_ref, block_ref, high_ref, low_ref), send_ref[send_ref.shape[0] - 1])


def tree(values):
    while len(values) > 1:
        values = [values[i] + values[i + 1] for i in range(0, len(values), 2)]
    return values[0]


def add_kernel(*refs):
    refs[-1][...] = tree([ref[...] for ref in refs[:-1]])


def join_kernel(keep_ref, got_ref, count_ref, other_ref, sum_ref, counts_ref):
    sum_ref[...] = keep_ref[...] + got_ref[...]
    counts_ref[...] = count_ref[...] + other_ref[...]


def middle_kernel(own_ref, one_ref, two_ref, three_ref, other_ref, sum_ref):
    count = own_ref.shape[0]
    for k in range(count):
        sum_ref[k] = tree([own_ref[k], one_ref[k], two_ref[k], three_ref[k]])
    for r in range(other_ref.shape[0]):
        sum_ref[count + r] = other_ref[r]


def weigh(c, across, projected, probability, scaled, weighted_ref):
    average = class_sum([projected[r] * probability[r] for r in range(2)])
    curve = jnp.zeros((SUB, LANE), f32)
    for r in range(2):
        value = scaled[r] * (projected[r] - average)
        weighted_ref[r * across + c] = value
        curve += projected[r] * value
    return curve


def softmax_kernel(
    place_ref,
    labels_ref,
    own_ref,
    one_ref,
    two_ref,
    three_ref,
    probability_ref,
    scaled_ref,
    first_ref,
    norm_ref,
    weighted_ref,
):
    def whole_sum(k):
        return tree([own_ref[k], one_ref[k], two_ref[k], three_ref[k]])

    across = first_ref.shape[0] // 2
    classes = 2 * SUB
    ids = lax.broadcasted_iota(jnp.int32, (SUB, LANE), 0)
    counts = [jnp.sum(whole_sum(4 * across + 1 + r), axis=1, keepdims=True) for r in range(2)]
    curve = jnp.zeros((SUB, LANE), f32)
    for c in range(across):
        powered = [jnp.exp(whole_sum(r * across + c)) for r in range(2)]
        projected = [whole_sum((2 + r) * across + c) for r in range(2)]
        whole = class_sum(powered)
        probability = [powered[r] / whole for r in range(2)]
        label = labels_ref[pl.ds((place_ref[0] & 1) * across + c, 1), :]
        own = class_sum([jnp.where(label == ids + r * SUB, counts[r], 0.0) for r in range(2)])
        scale = 1.0 / (classes * own)
        scaled = [scale * probability[r] for r in range(2)]
        for r in range(2):
            probability_ref[r * across + c] = probability[r]
            scaled_ref[r * across + c] = scaled[r]
            first_ref[r * across + c] = projected[r]
        curve += weigh(c, across, projected, probability, scaled, weighted_ref)
    weighted_ref[2 * across] = curve
    norm_ref[...] = jnp.broadcast_to(total(whole_sum(4 * across)), (SUB, LANE))


def second_kernel(pieces_ref, probability_ref, scaled_ref, first_ref, norm_ref, weighted_ref, numbers_ref):
    across = first_ref.shape[0] // 2
    sums = summed(pieces_ref, 2 * across)
    norm_next, cross = total(sums[:4]), total(sums[4:])
    norm_now = norm_ref[0:1, 0:1]
    ratio = norm_next / norm_now
    curve = jnp.zeros((SUB, LANE), f32)
    for c in range(across):
        projected, probability, scaled = [], [], []
        for r in range(2):
            i = r * across + c
            projected.append(summed(pieces_ref, i) + ratio * first_ref[i])
            probability.append(probability_ref[i])
            scaled.append(scaled_ref[i])
        curve += weigh(c, across, projected, probability, scaled, weighted_ref)
    weighted_ref[2 * across] = curve
    norm_direction = norm_next + ratio * (2.0 * cross + ratio * norm_now)
    for i, value in enumerate((norm_next, ratio, norm_direction)):
        numbers_ref[i] = jnp.broadcast_to(value, (SUB, LANE))


def put_together(weighted_ref, left_ref):
    across = (weighted_ref.shape[0] - 1) // 2
    classes = 2 * SUB
    for r in range(2):
        for c in range(across):
            high, low = parts(weighted_ref[r * across + c])
            at = slice(c * LANE, (c + 1) * LANE)
            left_ref[r * SUB : (r + 1) * SUB, at] = high.astype(f32)
            left_ref[classes + r * SUB : classes + (r + 1) * SUB, at] = low.astype(f32)
    return left_ref[...].astype(bf16)


def image_columns(at, step, left, high_ref, low_ref):
    classes = left.shape[0] // 2
    part = pl.ds(at, step)
    both = lax.dot_general(left, high_ref[:, part], ROWS_WITH_COLUMNS, preferred_element_type=f32)
    rest = lax.dot_general(left[:classes], low_ref[:, part], ROWS_WITH_COLUMNS, preferred_element_type=f32)
    return both[:classes] + both[classes:] + rest


def image_own_kernel(step, weighted_ref, high_ref, low_ref, image_ref, left_ref):
    left = put_together(weighted_ref, left_ref)
    for k in range(high_ref.shape[1] // step):
        image_ref[k] = image_columns(k * step, step, left, high_ref, low_ref)


def image_other_kernel(
    step, place_ref, other_ref, own_ref, high_ref, low_ref, before_ref, *piece_refs_and_left
):
    *piece_refs, left_ref = piece_refs_and_left
    last = own_ref.shape[0] - 1
    curve = own_ref[last] + other_ref[last]
    left = put_together(other_ref, left_ref)
    for d, piece_ref in enumerate(piece_refs):
        block = (place_ref[0] >> 1) ^ d
        at = pl.multiple_of(block * step, step)
        store_tiles(piece_ref, before_ref[block] + image_columns(at, step, left, high_ref, low_ref), curve)


def columns_of(piece_ref, classes):
    across = (piece_ref.shape[0] - 1) // (classes // SUB)
    rows = []
    for r in range(classes // SUB):
        rows.append(jnp.concatenate([piece_ref[r * across + c] for c in range(across)], axis=1))
    return jnp.concatenate(rows, axis=0)


def project_kept(left_ref, high_ref, low_ref):
    classes = left_ref.shape[0] // 2
    left = left_ref[...]
    both = lax.dot_general(left, high_ref[...], ROWS_WITH_ROWS, preferred_element_type=f32)
    rest = lax.dot_general(left[:classes], low_ref[...], ROWS_WITH_ROWS, preferred_element_type=f32)
    return both[:classes] + both[classes:] + rest


def residual_other_kernel(
    step,
    place_ref,
    own_ref,
    one_ref,
    two_ref,
    three_ref,
    norm_ref,
    right_ref,
    high_ref,
    low_ref,
    send_ref,
    residual_ref,
    rate_ref,
    left_ref,
):
    classes = right_ref.shape[0]
    norm_now = norm_ref[0:1, 0:1]
    curve = total(own_ref[own_ref.shape[0] - 1])
    rate = norm_now / (curve + ridge_strength * norm_now)
    rate_ref[...] = jnp.broadcast_to(rate, (SUB, LANE))
    for d, piece_ref in enumerate((own_ref, one_ref, two_ref, three_ref)):
        at = pl.ds(pl.multiple_of(((place_ref[0] >> 1) ^ d) * step, step), step)
        right = right_ref[:, at]
        residual = right - rate * (columns_of(piece_ref, classes) + ridge_strength * right)
        residual_ref[:, at] = residual
        high, low = parts(residual)
        left_ref[:classes, at] = high
        left_ref[classes:, at] = low
    right, residual = right_ref[...], residual_ref[...]
    norm, cross = fold(residual * residual), fold(residual * right)
    sums = jnp.concatenate([norm[:4] + norm[4:], cross[:4] + cross[4:]])
    store_tiles(send_ref, project_kept(left_ref, high_ref, low_ref), sums)


def residual_own_kernel(left_ref, high_ref, low_ref, send_ref, keep_ref):
    store_tiles(keep_ref, project_kept(left_ref, high_ref, low_ref), send_ref[send_ref.shape[0] - 1])


def last_kernel(
    step,
    place_ref,
    own_ref,
    one_ref,
    two_ref,
    three_ref,
    numbers_ref,
    rate_ref,
    right_ref,
    old_ref,
    solution_ref,
    residual_ref,
):
    classes = right_ref.shape[0]
    norm_next, ratio, norm_direction = [numbers_ref[i, 0:1, 0:1] for i in range(3)]
    curve = total(own_ref[own_ref.shape[0] - 1])
    rate = norm_next / (curve + ridge_strength * norm_direction)
    rate_first = rate_ref[0:1, 0:1]
    for d, piece_ref in enumerate((own_ref, one_ref, two_ref, three_ref)):
        at = pl.ds(pl.multiple_of(((place_ref[0] >> 1) ^ d) * step, step), step)
        right, old = right_ref[:, at], old_ref[:, at]
        direction = old + ratio * right
        image = columns_of(piece_ref, classes) + ridge_strength * direction
        solution_ref[:, at] = rate_first * right + rate * direction
        residual_ref[:, at] = old - rate * image


def on_device(features, labels, weights, right_side):
    classes, width = weights.shape
    tokens = features.shape[0]
    half = tokens // 2
    across = half // LANE
    groups = classes // SUB
    toks = lax.axis_size("tok")
    across_x, across_y = lax.axis_size("x"), lax.axis_size("y")
    labels = labels.reshape(tokens // LANE, LANE)
    step = width // 4
    tok = lax.axis_index("tok").astype(jnp.int32)
    role = (tok & 3) ^ (2 * (tok >> 2))
    place = (2 * role + lax.axis_index("core").astype(jnp.int32)).reshape(1)
    swap = [(0, 1), (1, 0)]
    half_product = pl.CostEstimate(
        flops=12 * classes * half * width, bytes_accessed=4 * half * width, transcendentals=0
    )
    reading = [pltpu.VMEM((width // step, half, step), f32), pltpu.SemaphoreType.DMA((width // step,))]
    kept_half = pltpu.VMEM((half, width), bf16)
    piece = tiles(groups * step // LANE + 1)
    put = pltpu.VMEM((2 * classes, half), f32)

    def with_step(kernel):
        return functools.partial(kernel, step)

    def swapped(value):
        return lax.ppermute(value, "core", swap)

    def from_tok(value, distances):
        pairs = [
            ((z + distances[y]) % toks * across_y + y, z * across_y + y)
            for z in range(toks)
            for y in range(across_y)
        ]
        return lax.ppermute(value, ("tok", "y"), pairs)

    def from_others(value, axis):
        values = value if isinstance(value, list) else [value] * 3
        count = lax.axis_size(axis)
        return [lax.ppermute(v, axis, [(i, i ^ (d + 1)) for i in range(count)]) for d, v in enumerate(values)]

    def add(name, *values):
        return call(add_kernel, name, [ON_CHIP] * len(values), tiles(values[0].shape[0]))(*values)

    def sum_over_tok(own, *rest):
        own = add("add_half", own, *from_others(list(rest), "tok"))
        own = add("add_tok", own, lax.ppermute(own, "tok", [(i, i ^ 6) for i in range(toks)]))
        return [own] + from_others(own, "tok")

    near, far = (-1, 2, 2, -1), (0, 1, 2, -2)
    kept = 2 * groups * across + 1
    send, count, left, high_other, low_other = call(
        with_step(first_other_kernel),
        "first_other",
        [SCALAR] + [IN_HBM] * 4,
        [tiles(kept), tiles(groups), pltpu.VMEM((4 * classes, width), bf16), kept_half, kept_half],
        [
            pltpu.VMEM(labels.shape, labels.dtype),
            pltpu.VMEM((classes, width), f32),
            pltpu.VMEM((classes, width), f32),
            reading[0],
            pltpu.SemaphoreType.DMA((3,)),
            reading[1],
        ],
        kib=61560 - 4096,
    )(place, labels, weights, right_side, features)
    got = swapped(send)
    other = from_tok(count, near)
    keep, high_own, low_own = call(
        with_step(first_own_kernel),
        "first_own",
        [SCALAR, ON_CHIP, ON_CHIP, IN_HBM],
        [tiles(kept), kept_half, kept_half],
        reading,
        mib=45,
        cost=half_product,
    )(place, left, send, features)

    own, count = call(join_kernel, "join", [ON_CHIP] * 4, [tiles(kept), tiles(groups)])(keep, got, count, other)
    others = from_others(own, "x")
    other = from_tok(count, far)
    own = call(middle_kernel, "middle", [ON_CHIP] * 5, tiles(kept + groups))(own, *others, other)
    others = from_others(own, "y")
    probability, scaled, first, norm_now, weighted = call(
        softmax_kernel,
        "softmax",
        [SCALAR] + [ON_CHIP] * 5,
        [tiles(groups * across)] * 3 + [tiles(), tiles(groups * across + 1)],
    )(place, labels, own, *others)

    def image(weighted):
        other = swapped(weighted)
        before = call(
            with_step(image_own_kernel),
            "image_own",
            [ON_CHIP] * 3,
            pltpu.VMEM((4, classes, step), f32),
            [put],
            cost=half_product,
        )(weighted, high_own, low_own)
        return call(
            with_step(image_other_kernel), "image_other", [SCALAR] + [ON_CHIP] * 5, [piece] * 4, [put]
        )(place, other, weighted, high_other, low_other, before)

    pieces = sum_over_tok(*image(weighted))

    kept = groups * across + 1
    send, residual, rate, left = call(
        with_step(residual_other_kernel),
        "residual_other",
        [SCALAR] + [ON_CHIP] * 8,
        [tiles(kept), pltpu.VMEM((classes, width), f32), tiles(), pltpu.VMEM((2 * classes, width), bf16)],
    )(place, *pieces, norm_now, right_side, high_other, low_other)
    got = swapped(send)
    keep = call(residual_own_kernel, "residual_own", [ON_CHIP] * 4, tiles(kept), cost=half_product)(
        left, high_own, low_own, send
    )
    own = add("add_core", keep, got)
    own = add("add_x", own, *from_others(own, "x"))
    own = add("add_y", own, *from_others(own, "y"))
    weighted, numbers = call(second_kernel, "second", [ON_CHIP] * 5, [tiles(kept), tiles(3)])(
        own[None], probability, scaled, first, norm_now
    )
    pieces = sum_over_tok(*image(weighted))
    out = jax.ShapeDtypeStruct((classes, width), f32)
    return tuple(
        call(with_step(last_kernel), "last", [SCALAR] + [ON_CHIP] * 8, [out, out])(
            place, *pieces, numbers, rate, right_side, residual
        )
    )


def solution(mesh):
    toks, feats = mesh.devices.shape
    across = math.isqrt(feats // 2)
    split = Mesh(mesh.devices.reshape(toks, across, across, 2), ("tok", "x", "y", "core"))
    feat = ("x", "y", "core")
    return jax.shard_map(
        on_device,
        mesh=split,
        in_specs=(P("tok", feat), P("tok"), P(None, feat), P(None, feat)),
        out_specs=(P(None, feat), P(None, feat)),
        check_vma=False,
    )
```

```python
import functools
import math

import jax
import jax.numpy as jnp
from jax import lax
from jax.experimental import pallas as pl
from jax.experimental.pallas import tpu as pltpu
from jax.sharding import Mesh, PartitionSpec as P

ridge_strength = 0.25
SUB, LANE = 8, 128
f32, bf16 = jnp.float32, jnp.bfloat16
ROWS_WITH_ROWS = (((1,), (1,)), ((), ()))
ROWS_WITH_COLUMNS = (((1,), (0,)), ((), ()))
ON_CHIP = pl.BlockSpec(memory_space=pltpu.VMEM)
SCALAR = pl.BlockSpec(memory_space=pltpu.SMEM)
IN_HBM = pl.BlockSpec(memory_space=pltpu.HBM)


def call(kernel, name, in_specs, outs, scratch=(), mib=8, kib=0, cost=None):
    return pl.pallas_call(
        kernel,
        out_shape=outs,
        in_specs=in_specs,
        out_specs=jax.tree.map(lambda _: ON_CHIP, outs),
        scratch_shapes=list(scratch),
        compiler_params=pltpu.CompilerParams(vmem_limit_bytes=kib << 10 if kib else mib << 20),
        cost_estimate=cost,
        name=name,
    )


def tiles(*lead):
    return pltpu.VMEM(lead + (SUB, LANE), f32)


def parts(x):
    high = x.astype(bf16)
    return high, (x - high.astype(f32)).astype(bf16)


def total(tile):
    return jnp.sum(tile, axis=(0, 1), keepdims=True)


def class_sum(pair):
    return jnp.sum(pair[0] + pair[1], axis=0, keepdims=True)


def fold(array):
    rows, columns = array.shape
    kept = None
    for r in range(rows // SUB):
        for c in range(columns // LANE):
            tile = array[r * SUB : (r + 1) * SUB, c * LANE : (c + 1) * LANE]
            kept = tile if kept is None else kept + tile
    return kept


def store_tiles(ref, value, extra):
    rows, columns = value.shape
    across = columns // LANE
    for r in range(rows // SUB):
        for c in range(across):
            ref[r * across + c] = value[r * SUB : (r + 1) * SUB, c * LANE : (c + 1) * LANE]
    ref[(rows // SUB) * across] = extra


def summed(pieces_ref, k):
    tile = pieces_ref[0, k]
    for i in range(1, pieces_ref.shape[0]):
        tile += pieces_ref[i, k]
    return tile


def read_half(row, step, features_ref, block_ref, sems):
    half, width = features_ref.shape[0] // 2, features_ref.shape[1]
    rows = pl.ds(pl.multiple_of(row, half), half)
    copies = []
    for k in range(width // step):
        copies.append(
            pltpu.make_async_copy(features_ref.at[rows, pl.ds(k * step, step)], block_ref.at[k], sems.at[k])
        )
        copies[-1].start()
    return copies


def project_half(copies, step, left_ref, block_ref, high_ref, low_ref):
    rows, half = left_ref.shape[0] // 2, block_ref.shape[1]
    both = jnp.zeros((2 * rows, half), f32)
    rest = jnp.zeros((rows, half), f32)
    for k, copy in enumerate(copies):
        part = slice(k * step, (k + 1) * step)
        copy.wait()
        high_ref[:, part], low_ref[:, part] = parts(block_ref[k])
        both += lax.dot_general(left_ref[:, part], high_ref[:, part], ROWS_WITH_ROWS, preferred_element_type=f32)
        rest += lax.dot_general(left_ref[:rows, part], low_ref[:, part], ROWS_WITH_ROWS, preferred_element_type=f32)
    return both[:rows] + both[rows:] + rest


def first_other_kernel(
    step,
    place_ref,
    labels_hbm,
    weights_hbm,
    right_hbm,
    features_ref,
    send_ref,
    count_ref,
    left_ref,
    high_ref,
    low_ref,
    labels_ref,
    weights_ref,
    right_ref,
    block_ref,
    sems,
    block_sems,
):
    pairs = ((weights_hbm, weights_ref), (right_hbm, right_ref), (labels_hbm, labels_ref))
    loads = [pltpu.make_async_copy(*pair, sems.at[i]) for i, pair in enumerate(pairs)]
    for load in loads:
        load.start()
    half = features_ref.shape[0] // 2
    copies = read_half((1 - (place_ref[0] & 1)) * half, step, features_ref, block_ref, block_sems)
    classes = weights_ref.shape[0]
    rows = 2 * classes
    for i, ref in enumerate((weights_ref, right_ref)):
        loads[i].wait()
        high, low = parts(ref[...])
        left_ref[i * classes : (i + 1) * classes] = high
        left_ref[rows + i * classes : rows + (i + 1) * classes] = low
    right = right_ref[...]
    norm = fold(right * right)
    loads[2].wait()
    ids = lax.broadcasted_iota(jnp.int32, (SUB, LANE), 0)
    for r in range(count_ref.shape[0]):
        count = jnp.zeros((SUB, LANE), f32)
        for row in range(labels_ref.shape[0]):
            count += (labels_ref[row : row + 1, :] == ids + r * SUB).astype(f32)
        count_ref[r] = count
    store_tiles(send_ref, project_half(copies, step, left_ref, block_ref, high_ref, low_ref), norm)


def first_own_kernel(
    step, place_ref, left_ref, send_ref, features_ref, keep_ref, high_ref, low_ref, block_ref, sems
):
    half = features_ref.shape[0] // 2
    copies = read_half((place_ref[0] & 1) * half, step, features_ref, block_ref, sems)
    store_tiles(keep_ref, project_half(copies, step, left_ref, block_ref, high_ref, low_ref), send_ref[send_ref.shape[0] - 1])


def tree(values):
    while len(values) > 1:
        values = [values[i] + values[i + 1] for i in range(0, len(values), 2)]
    return values[0]


def add_kernel(*refs):
    refs[-1][...] = tree([ref[...] for ref in refs[:-1]])


def join_kernel(keep_ref, got_ref, count_ref, other_ref, sum_ref, counts_ref):
    sum_ref[...] = keep_ref[...] + got_ref[...]
    counts_ref[...] = count_ref[...] + other_ref[...]


def middle_kernel(own_ref, one_ref, two_ref, three_ref, other_ref, sum_ref):
    count = own_ref.shape[0]
    for k in range(count):
        sum_ref[k] = tree([own_ref[k], one_ref[k], two_ref[k], three_ref[k]])
    for r in range(other_ref.shape[0]):
        sum_ref[count + r] = other_ref[r]


def weigh(c, across, projected, probability, scaled, weighted_ref):
    average = class_sum([projected[r] * probability[r] for r in range(2)])
    curve = jnp.zeros((SUB, LANE), f32)
    for r in range(2):
        value = scaled[r] * (projected[r] - average)
        weighted_ref[r * across + c] = value
        curve += projected[r] * value
    return curve


def softmax_kernel(
    place_ref,
    labels_ref,
    own_ref,
    one_ref,
    two_ref,
    three_ref,
    probability_ref,
    scaled_ref,
    first_ref,
    norm_ref,
    weighted_ref,
):
    def whole_sum(k):
        return tree([own_ref[k], one_ref[k], two_ref[k], three_ref[k]])

    across = first_ref.shape[0] // 2
    classes = 2 * SUB
    ids = lax.broadcasted_iota(jnp.int32, (SUB, LANE), 0)
    counts = [jnp.sum(whole_sum(4 * across + 1 + r), axis=1, keepdims=True) for r in range(2)]
    curve = jnp.zeros((SUB, LANE), f32)
    for c in range(across):
        powered = [jnp.exp(whole_sum(r * across + c)) for r in range(2)]
        projected = [whole_sum((2 + r) * across + c) for r in range(2)]
        whole = class_sum(powered)
        probability = [powered[r] / whole for r in range(2)]
        label = labels_ref[pl.ds((place_ref[0] & 1) * across + c, 1), :]
        own = class_sum([jnp.where(label == ids + r * SUB, counts[r], 0.0) for r in range(2)])
        scale = 1.0 / (classes * own)
        scaled = [scale * probability[r] for r in range(2)]
        for r in range(2):
            probability_ref[r * across + c] = probability[r]
            scaled_ref[r * across + c] = scaled[r]
            first_ref[r * across + c] = projected[r]
        curve += weigh(c, across, projected, probability, scaled, weighted_ref)
    weighted_ref[2 * across] = curve
    norm_ref[...] = jnp.broadcast_to(total(whole_sum(4 * across)), (SUB, LANE))


def second_kernel(pieces_ref, probability_ref, scaled_ref, first_ref, norm_ref, weighted_ref, numbers_ref):
    across = first_ref.shape[0] // 2
    sums = summed(pieces_ref, 2 * across)
    norm_next, cross = total(sums[:4]), total(sums[4:])
    norm_now = norm_ref[0:1, 0:1]
    ratio = norm_next / norm_now
    curve = jnp.zeros((SUB, LANE), f32)
    for c in range(across):
        projected, probability, scaled = [], [], []
        for r in range(2):
            i = r * across + c
            projected.append(summed(pieces_ref, i) + ratio * first_ref[i])
            probability.append(probability_ref[i])
            scaled.append(scaled_ref[i])
        curve += weigh(c, across, projected, probability, scaled, weighted_ref)
    weighted_ref[2 * across] = curve
    norm_direction = norm_next + ratio * (2.0 * cross + ratio * norm_now)
    for i, value in enumerate((norm_next, ratio, norm_direction)):
        numbers_ref[i] = jnp.broadcast_to(value, (SUB, LANE))


def put_together(weighted_ref, left_ref):
    across = (weighted_ref.shape[0] - 1) // 2
    classes = 2 * SUB
    for r in range(2):
        for c in range(across):
            high, low = parts(weighted_ref[r * across + c])
            at = slice(c * LANE, (c + 1) * LANE)
            left_ref[r * SUB : (r + 1) * SUB, at] = high.astype(f32)
            left_ref[classes + r * SUB : classes + (r + 1) * SUB, at] = low.astype(f32)
    return left_ref[...].astype(bf16)


def image_columns(at, step, left, high_ref, low_ref):
    classes = left.shape[0] // 2
    part = pl.ds(at, step)
    both = lax.dot_general(left, high_ref[:, part], ROWS_WITH_COLUMNS, preferred_element_type=f32)
    rest = lax.dot_general(left[:classes], low_ref[:, part], ROWS_WITH_COLUMNS, preferred_element_type=f32)
    return both[:classes] + both[classes:] + rest


def image_own_kernel(step, weighted_ref, high_ref, low_ref, image_ref, left_ref):
    left = put_together(weighted_ref, left_ref)
    for k in range(high_ref.shape[1] // step):
        image_ref[k] = image_columns(k * step, step, left, high_ref, low_ref)


def image_other_kernel(
    step, place_ref, other_ref, own_ref, high_ref, low_ref, before_ref, *piece_refs_and_left
):
    *piece_refs, left_ref = piece_refs_and_left
    last = own_ref.shape[0] - 1
    curve = own_ref[last] + other_ref[last]
    left = put_together(other_ref, left_ref)
    for d, piece_ref in enumerate(piece_refs):
        block = (place_ref[0] >> 1) ^ d
        at = pl.multiple_of(block * step, step)
        store_tiles(piece_ref, before_ref[block] + image_columns(at, step, left, high_ref, low_ref), curve)


def columns_of(piece_ref, classes):
    across = (piece_ref.shape[0] - 1) // (classes // SUB)
    rows = []
    for r in range(classes // SUB):
        rows.append(jnp.concatenate([piece_ref[r * across + c] for c in range(across)], axis=1))
    return jnp.concatenate(rows, axis=0)


def project_block(left, at, high_ref, low_ref):
    classes = left.shape[0] // 2
    both = lax.dot_general(left, high_ref[:, at], ROWS_WITH_ROWS, preferred_element_type=f32)
    rest = lax.dot_general(left[:classes], low_ref[:, at], ROWS_WITH_ROWS, preferred_element_type=f32)
    return both[:classes] + both[classes:] + rest


def block_at(step, place_ref, d):
    return pl.ds(pl.multiple_of(((place_ref[0] >> 1) ^ d) * step, step), step)


def residual_block(at, piece_ref, rate, right_ref, residual_ref, left_ref):
    classes = right_ref.shape[0]
    right = right_ref[:, at]
    residual = right - rate * (columns_of(piece_ref, classes) + ridge_strength * right)
    residual_ref[:, at] = residual
    high, low = parts(residual)
    left_ref[:classes, at] = high
    left_ref[classes:, at] = low


def residual_start_kernel(
    step,
    place_ref,
    own_ref,
    norm_ref,
    right_ref,
    high_own_ref,
    low_own_ref,
    high_other_ref,
    low_other_ref,
    rate_ref,
    residual_ref,
    share_own_ref,
    share_other_ref,
    left_ref,
):
    norm_now = norm_ref[0:1, 0:1]
    curve = total(own_ref[own_ref.shape[0] - 1])
    rate = norm_now / (curve + ridge_strength * norm_now)
    rate_ref[...] = jnp.broadcast_to(rate, (SUB, LANE))
    at = block_at(step, place_ref, 0)
    classes = right_ref.shape[0]
    right = right_ref[:, at]
    residual = right - rate * (columns_of(own_ref, classes) + ridge_strength * right)
    residual_ref[...] = residual
    high, low = parts(residual)
    left_ref[:classes] = high
    left_ref[classes:] = low
    left = left_ref[...]
    share_own_ref[...] = project_block(left, at, high_own_ref, low_own_ref)
    share_other_ref[...] = project_block(left, at, high_other_ref, low_other_ref)


def residual_other_kernel(
    step,
    place_ref,
    one_ref,
    two_ref,
    three_ref,
    rate_ref,
    start_ref,
    share_ref,
    right_ref,
    high_ref,
    low_ref,
    send_ref,
    residual_ref,
    left_ref,
):
    rate = rate_ref[0:1, 0:1]
    residual_ref[:, block_at(step, place_ref, 0)] = start_ref[...]
    for d, piece_ref in enumerate((one_ref, two_ref, three_ref)):
        residual_block(block_at(step, place_ref, d + 1), piece_ref, rate, right_ref, residual_ref, left_ref)
    right, residual = right_ref[...], residual_ref[...]
    norm, cross = fold(residual * residual), fold(residual * right)
    sums = jnp.concatenate([norm[:4] + norm[4:], cross[:4] + cross[4:]])
    value = share_ref[...]
    for d in range(1, 4):
        at = block_at(step, place_ref, d)
        value += project_block(left_ref[:, at], at, high_ref, low_ref)
    store_tiles(send_ref, value, sums)


def residual_own_kernel(step, place_ref, left_ref, share_ref, high_ref, low_ref, send_ref, keep_ref):
    value = share_ref[...]
    for d in range(1, 4):
        at = block_at(step, place_ref, d)
        value += project_block(left_ref[:, at], at, high_ref, low_ref)
    store_tiles(keep_ref, value, send_ref[send_ref.shape[0] - 1])


def finish_kernel(own_ref, numbers_ref, rate_ref, right_ref, old_ref, solution_ref, base_ref, last_rate_ref):
    norm_next, ratio, norm_direction = [numbers_ref[i, 0:1, 0:1] for i in range(3)]
    curve = total(own_ref[own_ref.shape[0] - 1])
    rate = norm_next / (curve + ridge_strength * norm_direction)
    right, old = right_ref[...], old_ref[...]
    direction = old + ratio * right
    solution_ref[...] = rate_ref[0:1, 0:1] * right + rate * direction
    base_ref[...] = old - rate * (ridge_strength * direction)
    last_rate_ref[...] = jnp.broadcast_to(rate, (SUB, LANE))


def last_kernel(step, place_ref, own_ref, one_ref, two_ref, three_ref, base_ref, rate_ref, residual_ref):
    classes = base_ref.shape[0]
    rate = rate_ref[0:1, 0:1]
    for d, piece_ref in enumerate((own_ref, one_ref, two_ref, three_ref)):
        at = pl.ds(pl.multiple_of(((place_ref[0] >> 1) ^ d) * step, step), step)
        residual_ref[:, at] = base_ref[:, at] - rate * columns_of(piece_ref, classes)


def on_device(features, labels, weights, right_side):
    classes, width = weights.shape
    tokens = features.shape[0]
    half = tokens // 2
    across = half // LANE
    groups = classes // SUB
    toks = lax.axis_size("tok")
    across_x, across_y = lax.axis_size("x"), lax.axis_size("y")
    labels = labels.reshape(tokens // LANE, LANE)
    step = width // 4
    tok = lax.axis_index("tok").astype(jnp.int32)
    role = jnp.minimum(tok, toks - 1 - tok)
    place = (2 * role + lax.axis_index("core").astype(jnp.int32)).reshape(1)
    swap = [(0, 1), (1, 0)]
    half_product = pl.CostEstimate(
        flops=12 * classes * half * width, bytes_accessed=4 * half * width, transcendentals=0
    )
    reading = [pltpu.VMEM((width // step, half, step), f32), pltpu.SemaphoreType.DMA((width // step,))]
    kept_half = pltpu.VMEM((half, width), bf16)
    piece = tiles(groups * step // LANE + 1)
    put = pltpu.VMEM((2 * classes, half), f32)

    def with_step(kernel):
        return functools.partial(kernel, step)

    def swapped(value):
        return lax.ppermute(value, "core", swap)

    def from_tok(value, distances):
        pairs = [
            ((z + distances[y]) % toks * across_y + y, z * across_y + y)
            for z in range(toks)
            for y in range(across_y)
        ]
        return lax.ppermute(value, ("tok", "y"), pairs)

    def from_others(value, axis):
        values = value if isinstance(value, list) else [value] * 3
        count = lax.axis_size(axis)
        return [lax.ppermute(v, axis, [(i, i ^ (d + 1)) for i in range(count)]) for d, v in enumerate(values)]

    def add(name, *values):
        return call(add_kernel, name, [ON_CHIP] * len(values), tiles(values[0].shape[0]))(*values)

    def sum_over_tok(own, *rest):
        own = add("add_half", own, *from_others(list(rest), "tok"))
        own = add("add_tok", own, lax.ppermute(own, "tok", [(i, toks - 1 - i) for i in range(toks)]))
        return [own] + from_others(own, "tok")

    near, far = (-1, 2, 2, -1), (0, 1, 2, -2)
    kept = 2 * groups * across + 1
    send, count, left, high_other, low_other = call(
        with_step(first_other_kernel),
        "first_other",
        [SCALAR] + [IN_HBM] * 4,
        [tiles(kept), tiles(groups), pltpu.VMEM((4 * classes, width), bf16), kept_half, kept_half],
        [
            pltpu.VMEM(labels.shape, labels.dtype),
            pltpu.VMEM((classes, width), f32),
            pltpu.VMEM((classes, width), f32),
            reading[0],
            pltpu.SemaphoreType.DMA((3,)),
            reading[1],
        ],
        kib=61560 - 4096,
    )(place, labels, weights, right_side, features)
    got = swapped(send)
    other = from_tok(count, near)
    keep, high_own, low_own = call(
        with_step(first_own_kernel),
        "first_own",
        [SCALAR, ON_CHIP, ON_CHIP, IN_HBM],
        [tiles(kept), kept_half, kept_half],
        reading,
        mib=45,
        cost=half_product,
    )(place, left, send, features)

    own, count = call(join_kernel, "join", [ON_CHIP] * 4, [tiles(kept), tiles(groups)])(keep, got, count, other)
    others = from_others(own, "x")
    other = from_tok(count, far)
    own = call(middle_kernel, "middle", [ON_CHIP] * 5, tiles(kept + groups))(own, *others, other)
    others = from_others(own, "y")
    probability, scaled, first, norm_now, weighted = call(
        softmax_kernel,
        "softmax",
        [SCALAR] + [ON_CHIP] * 5,
        [tiles(groups * across)] * 3 + [tiles(), tiles(groups * across + 1)],
    )(place, labels, own, *others)

    def image(weighted):
        other = swapped(weighted)
        before = call(
            with_step(image_own_kernel),
            "image_own",
            [ON_CHIP] * 3,
            pltpu.VMEM((4, classes, step), f32),
            [put],
            cost=half_product,
        )(weighted, high_own, low_own)
        return call(
            with_step(image_other_kernel), "image_other", [SCALAR] + [ON_CHIP] * 5, [piece] * 4, [put]
        )(place, other, weighted, high_other, low_other, before)

    pieces = sum_over_tok(*image(weighted))

    kept = groups * across + 1
    share = pltpu.VMEM((classes, half), f32)
    rate, start, share_own, share_other = call(
        with_step(residual_start_kernel),
        "residual_start",
        [SCALAR] + [ON_CHIP] * 7,
        [tiles(), pltpu.VMEM((classes, step), f32), share, share],
        [pltpu.VMEM((2 * classes, step), bf16)],
        cost=half_product,
    )(place, pieces[0], norm_now, right_side, high_own, low_own, high_other, low_other)
    send, residual, left = call(
        with_step(residual_other_kernel),
        "residual_other",
        [SCALAR] + [ON_CHIP] * 9,
        [tiles(kept), pltpu.VMEM((classes, width), f32), pltpu.VMEM((2 * classes, width), bf16)],
    )(place, *pieces[1:], rate, start, share_other, right_side, high_other, low_other)
    got = swapped(send)
    keep = call(
        with_step(residual_own_kernel), "residual_own", [SCALAR] + [ON_CHIP] * 5, tiles(kept), cost=half_product
    )(place, left, share_own, high_own, low_own, send)
    own = add("add_core", keep, got)
    own = add("add_x", own, *from_others(own, "x"))
    own = add("add_y", own, *from_others(own, "y"))
    weighted, numbers = call(second_kernel, "second", [ON_CHIP] * 5, [tiles(kept), tiles(3)])(
        own[None], probability, scaled, first, norm_now
    )
    pieces = sum_over_tok(*image(weighted))
    out = jax.ShapeDtypeStruct((classes, width), f32)
    solution, base, rate = call(
        finish_kernel,
        "finish",
        [ON_CHIP] * 5,
        [out, pltpu.VMEM((classes, width), f32), tiles()],
        cost=half_product,
    )(pieces[0], numbers, rate, right_side, residual)
    residual = call(with_step(last_kernel), "last", [SCALAR] + [ON_CHIP] * 6, out)(place, *pieces, base, rate)
    return solution, residual


def solution(mesh):
    toks, feats = mesh.devices.shape
    across = math.isqrt(feats // 2)
    split = Mesh(mesh.devices.reshape(toks, across, across, 2), ("tok", "x", "y", "core"))
    feat = ("x", "y", "core")
    return jax.shard_map(
        on_device,
        mesh=split,
        in_specs=(P("tok", feat), P("tok"), P(None, feat), P(None, feat)),
        out_specs=(P(None, feat), P(None, feat)),
        check_vma=False,
    )
```

```python
import functools
import math

import jax
import jax.numpy as jnp
from jax import lax
from jax.experimental import pallas as pl
from jax.experimental.pallas import tpu as pltpu
from jax.sharding import Mesh, PartitionSpec as P

ridge_strength = 0.25
SUB, LANE = 8, 128
f32, bf16 = jnp.float32, jnp.bfloat16
ROWS_WITH_ROWS = (((1,), (1,)), ((), ()))
ROWS_WITH_COLUMNS = (((1,), (0,)), ((), ()))
ON_CHIP = pl.BlockSpec(memory_space=pltpu.VMEM)
SCALAR = pl.BlockSpec(memory_space=pltpu.SMEM)
IN_HBM = pl.BlockSpec(memory_space=pltpu.HBM)


def call(kernel, name, in_specs, outs, scratch=(), mib=8, kib=0, cost=None):
    return pl.pallas_call(
        kernel,
        out_shape=outs,
        in_specs=in_specs,
        out_specs=jax.tree.map(lambda _: ON_CHIP, outs),
        scratch_shapes=list(scratch),
        compiler_params=pltpu.CompilerParams(vmem_limit_bytes=kib << 10 if kib else mib << 20),
        cost_estimate=cost,
        name=name,
    )


def tiles(*lead):
    return pltpu.VMEM(lead + (SUB, LANE), f32)


def parts(x):
    high = x.astype(bf16)
    return high, (x - high.astype(f32)).astype(bf16)


def total(tile):
    return jnp.sum(tile, axis=(0, 1), keepdims=True)


def class_sum(pair):
    return jnp.sum(pair[0] + pair[1], axis=0, keepdims=True)


def fold(array):
    rows, columns = array.shape
    kept = None
    for r in range(rows // SUB):
        for c in range(columns // LANE):
            tile = array[r * SUB : (r + 1) * SUB, c * LANE : (c + 1) * LANE]
            kept = tile if kept is None else kept + tile
    return kept


def store_tiles(ref, value, extra):
    rows, columns = value.shape
    across = columns // LANE
    for r in range(rows // SUB):
        for c in range(across):
            ref[r * across + c] = value[r * SUB : (r + 1) * SUB, c * LANE : (c + 1) * LANE]
    ref[(rows // SUB) * across] = extra


def summed(pieces_ref, k):
    tile = pieces_ref[0, k]
    for i in range(1, pieces_ref.shape[0]):
        tile += pieces_ref[i, k]
    return tile


def read_half(row, step, features_ref, block_ref, sems):
    half, width = features_ref.shape[0] // 2, features_ref.shape[1]
    rows = pl.ds(pl.multiple_of(row, half), half)
    copies = []
    for k in range(width // step):
        copies.append(
            pltpu.make_async_copy(features_ref.at[rows, pl.ds(k * step, step)], block_ref.at[k], sems.at[k])
        )
        copies[-1].start()
    return copies


def project_half(copies, step, left_ref, block_ref, high_ref, low_ref):
    rows, half = left_ref.shape[0] // 2, block_ref.shape[1]
    both = jnp.zeros((2 * rows, half), f32)
    rest = jnp.zeros((rows, half), f32)
    for k, copy in enumerate(copies):
        part = slice(k * step, (k + 1) * step)
        copy.wait()
        high_ref[:, part], low_ref[:, part] = parts(block_ref[k])
        both += lax.dot_general(left_ref[:, part], high_ref[:, part], ROWS_WITH_ROWS, preferred_element_type=f32)
        rest += lax.dot_general(left_ref[:rows, part], low_ref[:, part], ROWS_WITH_ROWS, preferred_element_type=f32)
    return both[:rows] + both[rows:] + rest


def first_other_kernel(
    step,
    place_ref,
    labels_hbm,
    weights_hbm,
    right_hbm,
    features_ref,
    send_ref,
    count_ref,
    left_ref,
    high_ref,
    low_ref,
    labels_ref,
    weights_ref,
    right_ref,
    block_ref,
    sems,
    block_sems,
):
    pairs = ((weights_hbm, weights_ref), (right_hbm, right_ref), (labels_hbm, labels_ref))
    loads = [pltpu.make_async_copy(*pair, sems.at[i]) for i, pair in enumerate(pairs)]
    for load in loads:
        load.start()
    half = features_ref.shape[0] // 2
    copies = read_half((1 - (place_ref[0] & 1)) * half, step, features_ref, block_ref, block_sems)
    classes = weights_ref.shape[0]
    rows = 2 * classes
    for i, ref in enumerate((weights_ref, right_ref)):
        loads[i].wait()
        high, low = parts(ref[...])
        left_ref[i * classes : (i + 1) * classes] = high
        left_ref[rows + i * classes : rows + (i + 1) * classes] = low
    right = right_ref[...]
    norm = fold(right * right)
    loads[2].wait()
    ids = lax.broadcasted_iota(jnp.int32, (SUB, LANE), 0)
    for r in range(count_ref.shape[0]):
        count = jnp.zeros((SUB, LANE), f32)
        for row in range(labels_ref.shape[0]):
            count += (labels_ref[row : row + 1, :] == ids + r * SUB).astype(f32)
        count_ref[r] = count
    store_tiles(send_ref, project_half(copies, step, left_ref, block_ref, high_ref, low_ref), norm)


def first_own_kernel(
    step, place_ref, left_ref, send_ref, features_ref, keep_ref, high_ref, low_ref, block_ref, sems
):
    half = features_ref.shape[0] // 2
    copies = read_half((place_ref[0] & 1) * half, step, features_ref, block_ref, sems)
    store_tiles(keep_ref, project_half(copies, step, left_ref, block_ref, high_ref, low_ref), send_ref[send_ref.shape[0] - 1])


def tree(values):
    while len(values) > 1:
        values = [values[i] + values[i + 1] for i in range(0, len(values), 2)]
    return values[0]


def add_kernel(*refs):
    refs[-1][...] = tree([ref[...] for ref in refs[:-1]])


def join_kernel(keep_ref, got_ref, count_ref, other_ref, sum_ref, counts_ref):
    sum_ref[...] = keep_ref[...] + got_ref[...]
    counts_ref[...] = count_ref[...] + other_ref[...]


def middle_kernel(own_ref, one_ref, two_ref, three_ref, other_ref, sum_ref):
    count = own_ref.shape[0]
    for k in range(count):
        sum_ref[k] = tree([own_ref[k], one_ref[k], two_ref[k], three_ref[k]])
    for r in range(other_ref.shape[0]):
        sum_ref[count + r] = other_ref[r]


def weigh(c, across, projected, probability, scaled, weighted_ref):
    average = class_sum([projected[r] * probability[r] for r in range(2)])
    curve = jnp.zeros((SUB, LANE), f32)
    for r in range(2):
        value = scaled[r] * (projected[r] - average)
        weighted_ref[r * across + c] = value
        curve += projected[r] * value
    return curve


def softmax_kernel(
    place_ref,
    labels_ref,
    own_ref,
    one_ref,
    two_ref,
    three_ref,
    probability_ref,
    scaled_ref,
    first_ref,
    norm_ref,
    weighted_ref,
):
    def whole_sum(k):
        return tree([own_ref[k], one_ref[k], two_ref[k], three_ref[k]])

    across = first_ref.shape[0] // 2
    classes = 2 * SUB
    ids = lax.broadcasted_iota(jnp.int32, (SUB, LANE), 0)
    counts = [jnp.sum(whole_sum(4 * across + 1 + r), axis=1, keepdims=True) for r in range(2)]
    curve = jnp.zeros((SUB, LANE), f32)
    for c in range(across):
        powered = [jnp.exp(whole_sum(r * across + c)) for r in range(2)]
        projected = [whole_sum((2 + r) * across + c) for r in range(2)]
        whole = class_sum(powered)
        probability = [powered[r] / whole for r in range(2)]
        label = labels_ref[pl.ds((place_ref[0] & 1) * across + c, 1), :]
        own = class_sum([jnp.where(label == ids + r * SUB, counts[r], 0.0) for r in range(2)])
        scale = 1.0 / (classes * own)
        scaled = [scale * probability[r] for r in range(2)]
        for r in range(2):
            probability_ref[r * across + c] = probability[r]
            scaled_ref[r * across + c] = scaled[r]
            first_ref[r * across + c] = projected[r]
        curve += weigh(c, across, projected, probability, scaled, weighted_ref)
    weighted_ref[2 * across] = curve
    norm_ref[...] = jnp.broadcast_to(total(whole_sum(4 * across)), (SUB, LANE))


def second_kernel(pieces_ref, probability_ref, scaled_ref, first_ref, norm_ref, weighted_ref, numbers_ref):
    across = first_ref.shape[0] // 2
    sums = summed(pieces_ref, 2 * across)
    norm_next, cross = total(sums[:4]), total(sums[4:])
    norm_now = norm_ref[0:1, 0:1]
    ratio = norm_next / norm_now
    curve = jnp.zeros((SUB, LANE), f32)
    for c in range(across):
        projected, probability, scaled = [], [], []
        for r in range(2):
            i = r * across + c
            projected.append(summed(pieces_ref, i) + ratio * first_ref[i])
            probability.append(probability_ref[i])
            scaled.append(scaled_ref[i])
        curve += weigh(c, across, projected, probability, scaled, weighted_ref)
    weighted_ref[2 * across] = curve
    norm_direction = norm_next + ratio * (2.0 * cross + ratio * norm_now)
    for i, value in enumerate((norm_next, ratio, norm_direction)):
        numbers_ref[i] = jnp.broadcast_to(value, (SUB, LANE))


def put_together(weighted_ref, left_ref):
    across = (weighted_ref.shape[0] - 1) // 2
    classes = 2 * SUB
    for r in range(2):
        for c in range(across):
            high, low = parts(weighted_ref[r * across + c])
            at = slice(c * LANE, (c + 1) * LANE)
            left_ref[r * SUB : (r + 1) * SUB, at] = high.astype(f32)
            left_ref[classes + r * SUB : classes + (r + 1) * SUB, at] = low.astype(f32)
    return left_ref[...].astype(bf16)


def image_columns(at, step, left, high_ref, low_ref):
    classes = left.shape[0] // 2
    part = pl.ds(at, step)
    both = lax.dot_general(left, high_ref[:, part], ROWS_WITH_COLUMNS, preferred_element_type=f32)
    rest = lax.dot_general(left[:classes], low_ref[:, part], ROWS_WITH_COLUMNS, preferred_element_type=f32)
    return both[:classes] + both[classes:] + rest


def image_own_kernel(step, weighted_ref, high_ref, low_ref, image_ref, left_ref):
    left = put_together(weighted_ref, left_ref)
    for k in range(high_ref.shape[1] // step):
        image_ref[k] = image_columns(k * step, step, left, high_ref, low_ref)


def image_other_kernel(
    step, wanted, place_ref, other_ref, own_ref, high_ref, low_ref, before_ref, *piece_refs_and_left
):
    *piece_refs, left_ref = piece_refs_and_left
    last = own_ref.shape[0] - 1
    curve = own_ref[last] + other_ref[last]
    left = put_together(other_ref, left_ref)
    for d, piece_ref in zip(wanted, piece_refs, strict=True):
        block = (place_ref[0] >> 1) ^ d
        at = pl.multiple_of(block * step, step)
        store_tiles(piece_ref, before_ref[block] + image_columns(at, step, left, high_ref, low_ref), curve)


def columns_of(piece_ref, classes):
    across = (piece_ref.shape[0] - 1) // (classes // SUB)
    rows = []
    for r in range(classes // SUB):
        rows.append(jnp.concatenate([piece_ref[r * across + c] for c in range(across)], axis=1))
    return jnp.concatenate(rows, axis=0)


def project_block(left, at, high_ref, low_ref):
    classes = left.shape[0] // 2
    both = lax.dot_general(left, high_ref[:, at], ROWS_WITH_ROWS, preferred_element_type=f32)
    rest = lax.dot_general(left[:classes], low_ref[:, at], ROWS_WITH_ROWS, preferred_element_type=f32)
    return both[:classes] + both[classes:] + rest


def block_at(step, place_ref, d):
    return pl.ds(pl.multiple_of(((place_ref[0] >> 1) ^ d) * step, step), step)


def residual_block(at, piece_ref, rate, right_ref, residual_ref, left_ref):
    classes = right_ref.shape[0]
    right = right_ref[:, at]
    residual = right - rate * (columns_of(piece_ref, classes) + ridge_strength * right)
    residual_ref[:, at] = residual
    high, low = parts(residual)
    left_ref[:classes, at] = high
    left_ref[classes:, at] = low


def residual_start_kernel(
    step,
    place_ref,
    own_ref,
    norm_ref,
    right_ref,
    high_own_ref,
    low_own_ref,
    high_other_ref,
    low_other_ref,
    rate_ref,
    residual_ref,
    share_own_ref,
    share_other_ref,
    left_ref,
):
    norm_now = norm_ref[0:1, 0:1]
    curve = total(own_ref[own_ref.shape[0] - 1])
    rate = norm_now / (curve + ridge_strength * norm_now)
    rate_ref[...] = jnp.broadcast_to(rate, (SUB, LANE))
    at = block_at(step, place_ref, 0)
    classes = right_ref.shape[0]
    right = right_ref[:, at]
    residual = right - rate * (columns_of(own_ref, classes) + ridge_strength * right)
    residual_ref[...] = residual
    high, low = parts(residual)
    left_ref[:classes] = high
    left_ref[classes:] = low
    left = left_ref[...]
    share_own_ref[...] = project_block(left, at, high_own_ref, low_own_ref)
    share_other_ref[...] = project_block(left, at, high_other_ref, low_other_ref)


def residual_other_kernel(
    step,
    place_ref,
    one_ref,
    two_ref,
    three_ref,
    rate_ref,
    start_ref,
    share_ref,
    right_ref,
    high_ref,
    low_ref,
    send_ref,
    residual_ref,
    left_ref,
):
    rate = rate_ref[0:1, 0:1]
    residual_ref[:, block_at(step, place_ref, 0)] = start_ref[...]
    for d, piece_ref in enumerate((one_ref, two_ref, three_ref)):
        residual_block(block_at(step, place_ref, d + 1), piece_ref, rate, right_ref, residual_ref, left_ref)
    right, residual = right_ref[...], residual_ref[...]
    norm, cross = fold(residual * residual), fold(residual * right)
    sums = jnp.concatenate([norm[:4] + norm[4:], cross[:4] + cross[4:]])
    value = share_ref[...]
    for d in range(1, 4):
        at = block_at(step, place_ref, d)
        value += project_block(left_ref[:, at], at, high_ref, low_ref)
    store_tiles(send_ref, value, sums)


def residual_own_kernel(step, place_ref, left_ref, share_ref, high_ref, low_ref, send_ref, keep_ref):
    value = share_ref[...]
    for d in range(1, 4):
        at = block_at(step, place_ref, d)
        value += project_block(left_ref[:, at], at, high_ref, low_ref)
    store_tiles(keep_ref, value, send_ref[send_ref.shape[0] - 1])


def finish_kernel(own_ref, numbers_ref, rate_ref, right_ref, old_ref, solution_ref, base_ref, last_rate_ref):
    norm_next, ratio, norm_direction = [numbers_ref[i, 0:1, 0:1] for i in range(3)]
    curve = total(own_ref[own_ref.shape[0] - 1])
    rate = norm_next / (curve + ridge_strength * norm_direction)
    right, old = right_ref[...], old_ref[...]
    direction = old + ratio * right
    solution_ref[...] = rate_ref[0:1, 0:1] * right + rate * direction
    base_ref[...] = old - rate * (ridge_strength * direction)
    last_rate_ref[...] = jnp.broadcast_to(rate, (SUB, LANE))


def last_kernel(step, place_ref, own_ref, one_ref, two_ref, three_ref, base_ref, rate_ref, residual_ref):
    classes = base_ref.shape[0]
    rate = rate_ref[0:1, 0:1]
    for d, piece_ref in enumerate((own_ref, one_ref, two_ref, three_ref)):
        at = pl.ds(pl.multiple_of(((place_ref[0] >> 1) ^ d) * step, step), step)
        residual_ref[:, at] = base_ref[:, at] - rate * columns_of(piece_ref, classes)


def on_device(features, labels, weights, right_side):
    classes, width = weights.shape
    tokens = features.shape[0]
    half = tokens // 2
    across = half // LANE
    groups = classes // SUB
    toks = lax.axis_size("tok")
    across_x, across_y = lax.axis_size("x"), lax.axis_size("y")
    labels = labels.reshape(tokens // LANE, LANE)
    step = width // 4
    tok = lax.axis_index("tok").astype(jnp.int32)
    role = jnp.minimum(tok, toks - 1 - tok)
    place = (2 * role + lax.axis_index("core").astype(jnp.int32)).reshape(1)
    swap = [(0, 1), (1, 0)]
    half_product = pl.CostEstimate(
        flops=12 * classes * half * width, bytes_accessed=4 * half * width, transcendentals=0
    )
    reading = [pltpu.VMEM((width // step, half, step), f32), pltpu.SemaphoreType.DMA((width // step,))]
    kept_half = pltpu.VMEM((half, width), bf16)
    piece = tiles(groups * step // LANE + 1)
    put = pltpu.VMEM((2 * classes, half), f32)

    def with_step(kernel):
        return functools.partial(kernel, step)

    def swapped(value):
        return lax.ppermute(value, "core", swap)

    def from_tok(value, distances):
        pairs = [
            ((z + distances[y]) % toks * across_y + y, z * across_y + y)
            for z in range(toks)
            for y in range(across_y)
        ]
        return lax.ppermute(value, ("tok", "y"), pairs)

    def from_others(value, axis):
        values = value if isinstance(value, list) else [value] * 3
        count = lax.axis_size(axis)
        return [lax.ppermute(v, axis, [(i, i ^ (d + 1)) for i in range(count)]) for d, v in enumerate(values)]

    def add(name, *values):
        return call(add_kernel, name, [ON_CHIP] * len(values), tiles(values[0].shape[0]))(*values)

    def sum_over_tok(own, *rest):
        own = add("add_half", own, *from_others(list(rest), "tok"))
        own = add("add_tok", own, lax.ppermute(own, "tok", [(i, toks - 1 - i) for i in range(toks)]))
        return [own] + from_others(own, "tok")

    near, far = (-1, 2, 2, -1), (0, 1, 2, -2)
    kept = 2 * groups * across + 1
    send, count, left, high_other, low_other = call(
        with_step(first_other_kernel),
        "first_other",
        [SCALAR] + [IN_HBM] * 4,
        [tiles(kept), tiles(groups), pltpu.VMEM((4 * classes, width), bf16), kept_half, kept_half],
        [
            pltpu.VMEM(labels.shape, labels.dtype),
            pltpu.VMEM((classes, width), f32),
            pltpu.VMEM((classes, width), f32),
            reading[0],
            pltpu.SemaphoreType.DMA((3,)),
            reading[1],
        ],
        kib=61560 - 4096,
    )(place, labels, weights, right_side, features)
    got = swapped(send)
    other = from_tok(count, near)
    keep, high_own, low_own = call(
        with_step(first_own_kernel),
        "first_own",
        [SCALAR, ON_CHIP, ON_CHIP, IN_HBM],
        [tiles(kept), kept_half, kept_half],
        reading,
        mib=45,
        cost=half_product,
    )(place, left, send, features)

    own, count = call(join_kernel, "join", [ON_CHIP] * 4, [tiles(kept), tiles(groups)])(keep, got, count, other)
    others = from_others(own, "x")
    other = from_tok(count, far)
    own = call(middle_kernel, "middle", [ON_CHIP] * 5, tiles(kept + groups))(own, *others, other)
    others = from_others(own, "y")
    probability, scaled, first, norm_now, weighted = call(
        softmax_kernel,
        "softmax",
        [SCALAR] + [ON_CHIP] * 5,
        [tiles(groups * across)] * 3 + [tiles(), tiles(groups * across + 1)],
    )(place, labels, own, *others)

    def image(weighted):
        other = swapped(weighted)
        before = call(
            with_step(image_own_kernel),
            "image_own",
            [ON_CHIP] * 3,
            pltpu.VMEM((4, classes, step), f32),
            [put],
            cost=half_product,
        )(weighted, high_own, low_own)

        def image_pieces(wanted, name, cost=None):
            return call(
                functools.partial(image_other_kernel, step, wanted),
                name,
                [SCALAR] + [ON_CHIP] * 5,
                [piece] * len(wanted),
                [put],
                cost=cost,
            )(place, other, weighted, high_other, low_other, before)

        pieces = image_pieces((1, 2, 3), "image_send")
        return image_pieces((0,), "image_keep", half_product) + pieces

    pieces = sum_over_tok(*image(weighted))

    kept = groups * across + 1
    share = pltpu.VMEM((classes, half), f32)
    rate, start, share_own, share_other = call(
        with_step(residual_start_kernel),
        "residual_start",
        [SCALAR] + [ON_CHIP] * 7,
        [tiles(), pltpu.VMEM((classes, step), f32), share, share],
        [pltpu.VMEM((2 * classes, step), bf16)],
        cost=half_product,
    )(place, pieces[0], norm_now, right_side, high_own, low_own, high_other, low_other)
    send, residual, left = call(
        with_step(residual_other_kernel),
        "residual_other",
        [SCALAR] + [ON_CHIP] * 9,
        [tiles(kept), pltpu.VMEM((classes, width), f32), pltpu.VMEM((2 * classes, width), bf16)],
    )(place, *pieces[1:], rate, start, share_other, right_side, high_other, low_other)
    got = swapped(send)
    keep = call(
        with_step(residual_own_kernel), "residual_own", [SCALAR] + [ON_CHIP] * 5, tiles(kept), cost=half_product
    )(place, left, share_own, high_own, low_own, send)
    own = add("add_core", keep, got)
    own = add("add_x", own, *from_others(own, "x"))
    own = add("add_y", own, *from_others(own, "y"))
    weighted, numbers = call(second_kernel, "second", [ON_CHIP] * 5, [tiles(kept), tiles(3)])(
        own[None], probability, scaled, first, norm_now
    )
    pieces = sum_over_tok(*image(weighted))
    out = jax.ShapeDtypeStruct((classes, width), f32)
    solution, base, rate = call(
        finish_kernel,
        "finish",
        [ON_CHIP] * 5,
        [out, pltpu.VMEM((classes, width), f32), tiles()],
        cost=half_product,
    )(pieces[0], numbers, rate, right_side, residual)
    residual = call(with_step(last_kernel), "last", [SCALAR] + [ON_CHIP] * 6, out)(place, *pieces, base, rate)
    return solution, residual


def solution(mesh):
    toks, feats = mesh.devices.shape
    across = math.isqrt(feats // 2)
    split = Mesh(mesh.devices.reshape(toks, across, across, 2), ("tok", "x", "y", "core"))
    feat = ("x", "y", "core")
    return jax.shard_map(
        on_device,
        mesh=split,
        in_specs=(P("tok", feat), P("tok"), P(None, feat), P(None, feat)),
        out_specs=(P(None, feat), P(None, feat)),
        check_vma=False,
    )
```
